256 devices in a mesh: row: 16 (over z_lo, x, core), col: 16 (over y, z_hi).
Axes of the slice: x: 4, y: 4, z: 8 (z_hi: 4, z_lo: 2; z = z_hi * 2 + z_lo), core: 2. Of those that a mesh axis runs over, the one named last changes fastest.
Arguments:
- embeddings: bfloat16 [384, 65536], P(None, ('row', 'col')), may hold values from -6 to 6
- solution: float32 [16, 65536], P(None, ('row', 'col')), may hold values from -6 to 6
- residual: float32 [16, 65536], P(None, ('row', 'col')), may hold values from -6 to 6
- direction: float32 [16, 65536], P(None, ('row', 'col')), may hold values from -6 to 6
Outputs:
- solution_next: float32 [16, 65536], P(None, ('row', 'col'))
- residual_next: float32 [16, 65536], P(None, ('row', 'col'))
- direction_next: float32 [16, 65536], P(None, ('row', 'col'))
The draws below stay inside these ranges and needn't reach their ends.
All inputs are finite; a program needn't handle non-finite values.
Results may differ from the reference program's by a relative error of at most 0.0003.
Values may be sent and summed in bfloat16 or wider, within the bound.
A program may use at most 64 MiB of HBM per device.

```python
import math
import jax
import jax.numpy as jnp
from jax import lax

D = 384
RUBRICS = 16
N = 65536


def block_levels(key, shape, cuts, least, high):
    gain, own = 1.0, jax.random.fold_in(key, 6)
    for position, shards_of in cuts:
        steps = jnp.exp(jax.random.uniform(jax.random.fold_in(own, position), (shards_of,), jnp.float32, least / len(cuts), high / len(cuts)))
        gain = gain * jnp.repeat(steps, shape[position] // shards_of).reshape([-1 if axis == position else 1 for axis in range(len(shape))])
    return gain


def scatter_about(own_key, extent, width, most, split=(), held_as=jnp.bfloat16):
    entries = width * jax.random.normal(own_key, extent, jnp.float32)
    if split:
        entries = entries * block_levels(own_key, extent, split, -0.22, 0.18)
    return jnp.clip(entries, -most, most).astype(held_as)


def setup_inputs(seed: int = 0) -> dict:
    streams_of = jax.random.split(jax.random.key(seed), 5)
    embeddings = scatter_about(streams_of[0], (D, N), 1.0, 6.0, ((1, 256),))
    solution = scatter_about(streams_of[1], (RUBRICS, N), 1.0, 6.0, ((1, 256),), jnp.float32)
    residual = scatter_about(streams_of[2], (RUBRICS, N), 1.0, 6.0, ((1, 256),), jnp.float32)
    direction = scatter_about(streams_of[3], (RUBRICS, N), 1.0, 6.0, ((1, 256),), jnp.float32)
    return dict(embeddings=embeddings, solution=solution, residual=residual, direction=direction)


ridge_weight = 0.5
highest = lax.Precision.HIGHEST

def column_squares(values):
    floats = values.astype(jnp.float32)
    return jnp.sum(floats * floats, axis=0)

def spd_solve(matrix, right):
    factor = jnp.linalg.cholesky(matrix)
    middle = lax.linalg.triangular_solve(factor, right, left_side=True, lower=True)
    return lax.linalg.triangular_solve(factor, middle, left_side=True, lower=True, transpose_a=True)

def reference(embeddings, solution, residual, direction):
    feature_width = embeddings.shape[0]
    count_all = embeddings.shape[1]
    span = math.gcd(count_all, 2048)
    all_sq = column_squares(embeddings)
    blocks = embeddings.reshape(feature_width, count_all // span, span).transpose(1, 0, 2)
    block_sq = all_sq.reshape(count_all // span, span)

    def block_product(inputs):
        block_rows, block_norms = inputs
        cross = jnp.dot(block_rows.T.astype(jnp.float32), embeddings.astype(jnp.float32), preferred_element_type=jnp.float32)
        distance = block_norms[:, None] + all_sq[None, :] - 2.0 * cross
        kernel = jnp.exp(distance * (-2.0 / feature_width))
        return jnp.dot(direction, kernel.T, precision=highest)
    pieces = lax.map(block_product, (blocks, block_sq))
    applied = pieces.transpose(1, 0, 2).reshape(direction.shape[0], count_all)
    product = applied + ridge_weight * direction
    curvature = jnp.dot(direction, product.T, precision=highest)
    curvature = 0.5 * (curvature + curvature.T)
    old_gram = jnp.dot(residual, residual.T, precision=highest)
    alpha_mat = spd_solve(curvature, old_gram)
    solution_next = solution + jnp.dot(alpha_mat.T, direction, precision=highest)
    residual_next = residual - jnp.dot(alpha_mat.T, product, precision=highest)
    new_gram = jnp.dot(residual_next, residual_next.T, precision=highest)
    beta_mat = spd_solve(old_gram, new_gram)
    direction_next = residual_next + jnp.dot(beta_mat.T, direction, precision=highest)
    return (solution_next, residual_next, direction_next)
```

```python
import functools

import jax
import jax.numpy as jnp
from jax import lax
from jax.experimental import pallas as pl
from jax.experimental.pallas import tpu as pltpu
from jax.sharding import PartitionSpec as P

f32, bf16, f8 = jnp.float32, jnp.bfloat16, jnp.float8_e4m3fn
MESH = pl.DeviceIdType.MESH
highest = lax.Precision.HIGHEST

ridge_weight = 0.5
points = 256
rubrics = 16
width = 384
deep = 512
aug_at, hi_at, lo_at, rows_sent = 384, 400, 416, 432
low_scale, dir_scale, dir_step = 65536.0, 64.0, 16.0
scale = 4.0 / width

slots = [
    ((1, 0), (1, 0)),
    ((0, 3), (0, 3)),
    ((1, 3), (1, 0)),
    ((1, 1), (0, 1)),
    ((2, 1), (1, 0)),
    ((3, 2), (3, 0)),
    ((2, 0), (0, 3)),
    ((0, 2), (0, 3)),
    ((0, 0), None),
    ((2, 2), (0, 1)),
]
own = 8
place = {offset: index for index, (offset, _) in enumerate(slots)}
along_z = [0, 1, 7, 2, 6, 3, 5, 4]
half_rows = 208
tiles = 34


def parent(index):
    (ox, oy), (hx, hy) = slots[index]
    return place[((ox - hx) % 4, (oy - hy) % 4)]


def tile_at(t):
    late = t - 21
    i = jnp.where(t < 5, 0, 1)
    k = jnp.where(t < 5, t, t - 5)
    i = jnp.where(t >= 10, 2, i)
    k = jnp.where(t >= 10, t - 10, k)
    i = jnp.where(t >= 15, t - 15, i)
    k = jnp.where(t >= 15, 6, k)
    i = jnp.where(t >= 18, t - 18, i)
    k = jnp.where(t >= 18, 5, k)
    i = jnp.where(t >= 21, 3 + lax.rem(late, 2), i)
    k = jnp.where(t >= 21, jnp.maximum(2 * lax.div(late, 2) - 1, 0), k)
    i = jnp.where(t >= 29, t - 29, i)
    k = jnp.where(t >= 29, 7, k)
    last = t >= tiles
    return jnp.where(last, 0, i), jnp.where(last, 0, k)


def nt(left, right, precision=None):
    return lax.dot_general(
        left, right, (((1,), (1,)), ((), ())), precision=precision, preferred_element_type=f32
    )


def nn(left, right):
    return jnp.dot(left, right, precision=highest, preferred_element_type=f32)


def low_parts(pieces):
    whole = pieces.astype(f32)
    whole = (whole[:rubrics] + whole[rubrics:]) * dir_scale
    first = whole.astype(f8)
    second = ((whole - first.astype(f32)) * dir_step).astype(f8)
    return jnp.concatenate([first, second], axis=0)


def combine(parts):
    low = parts[32:48] + parts[48:64] * (1.0 / dir_step)
    return parts[0:16] + parts[16:32] + low * (1.0 / (low_scale * dir_scale))


def inverse(matrix):
    size = matrix.shape[0]
    row = lax.broadcasted_iota(jnp.int32, matrix.shape, 0)
    col = lax.broadcasted_iota(jnp.int32, matrix.shape, 1)
    for step in range(size):
        pivot_row = matrix[step : step + 1, :]
        pivot_col = matrix[:, step : step + 1]
        pivot = 1.0 / matrix[step : step + 1, step : step + 1]
        scaled = pivot_row * pivot
        inner = matrix - pivot_col * scaled
        at_row, at_col = row == step, col == step
        matrix = jnp.where(
            at_row,
            jnp.where(at_col, pivot, scaled),
            jnp.where(at_col, -pivot_col * pivot, inner),
        )
    return matrix


def kernel(
    e_ref, sol_ref, res_ref, dir_ref, sol_out, res_out, dir_out,
    xb, xa, la, acc_a, acc_b, s0, s1, part_a, part_b, sum_a, sum_b, gram, gram_xy, gram_zc,
    a_send, a_recv, z_send, z_recv, c_send, c_recv, pa_send, pa_recv, pb_send, pb_recv, g_send, g_recv,
):
    row, col = lax.axis_index("row"), lax.axis_index("col")
    core, x, z_lo = lax.rem(row, 2), lax.rem(lax.div(row, 2), 4), lax.div(row, 8)
    y, z_hi = lax.div(col, 4), lax.rem(col, 4)
    z = z_hi * 2 + z_lo

    def device(dx=0, dy=0, dz=0, dc=0):
        x2, y2 = lax.rem(x + dx % 4, 4), lax.rem(y + dy % 4, 4)
        z2, c2 = lax.rem(z + dz % 8, 8), lax.rem(core + dc, 2)
        return (lax.rem(z2, 2) * 8 + x2 * 2 + c2, y2 * 4 + lax.div(z2, 2))

    plane = [(o // 4, o % 4) for o in range(1, 16)]
    column = [(o // 2, o % 2) for o in range(1, 16)]

    barrier = pltpu.get_barrier_semaphore()
    for dx, dy in plane:
        pl.semaphore_signal(barrier, inc=1, device_id=device(dx=dx, dy=dy), device_id_type=MESH)
    for dz, dc in column:
        pl.semaphore_signal(barrier, inc=1, device_id=device(dz=dz, dc=dc), device_id_type=MESH)

    block = e_ref[...]
    wide = block.astype(f32)
    half = -0.5 * jnp.sum(wide * wide, axis=0, keepdims=True)
    h1 = half.astype(bf16).astype(f32)
    h2 = (half - h1).astype(bf16).astype(f32)
    h3 = half - h1 - h2
    at = lax.broadcasted_iota(jnp.int32, (16, points), 0)
    ones = jnp.where((at >= 8) & (at < 11), 1.0, 0.0)
    aug = jnp.where(at == 0, h1, jnp.where(at == 1, h2, jnp.where(at == 2, h3, ones)))
    way = dir_ref[...]
    way_hi = way.astype(bf16)
    way_lo = (way - way_hi.astype(f32)).astype(bf16)
    for buffer, slot in ((xb, 0), (xa, own)):
        buffer[slot, 0:width, :] = block
        buffer[slot, aug_at:hi_at, :] = aug.astype(bf16)
        buffer[slot, hi_at:lo_at, :] = way_hi
        buffer[slot, lo_at:rows_sent, :] = way_lo

    pl.semaphore_wait(barrier, 30)

    body_rows = pl.ds(0, rows_sent)

    def a_copy(index):
        hx, hy = slots[index][1]
        return pltpu.make_async_remote_copy(
            src_ref=xa.at[parent(index)], dst_ref=xa.at[index],
            send_sem=a_send.at[index], recv_sem=a_recv.at[index],
            device_id=device(dx=-hx, dy=-hy), device_id_type=MESH,
        )

    def z_copy(index):
        slot = min(index, 7)
        source = [None, 0, 0, 1, 2, 3, 4, 5, 6][index]
        rows = body_rows
        if index == 7:
            rows = pl.ds(0, half_rows)
        if index == 8:
            rows = pl.ds(half_rows, rows_sent - half_rows)
        step = -1 if index in (1, 3, 5, 7) else 1
        return pltpu.make_async_remote_copy(
            src_ref=xb.at[2 * source, rows, :], dst_ref=xb.at[2 * slot, rows, :],
            send_sem=z_send.at[index], recv_sem=z_recv.at[index],
            device_id=device(dz=step), device_id_type=MESH,
        )

    def c_copy(slot):
        return pltpu.make_async_remote_copy(
            src_ref=xb.at[2 * slot, body_rows, :], dst_ref=xb.at[2 * slot + 1, body_rows, :],
            send_sem=c_send.at[slot], recv_sem=c_recv.at[slot],
            device_id=device(dc=1), device_id_type=MESH,
        )

    def turn(index):
        rows = pl.ds(index * points, points)
        la[rows, 0:width] = xa[index, 0:width, :].T
        extra = xa[index, aug_at:hi_at, :].astype(f32)
        extra = jnp.concatenate([extra[8:16], extra[0:8], jnp.zeros((112, points), f32)], axis=0)
        la[rows, width:deep] = extra.T.astype(bf16)

    for index in (0, 1):
        a_copy(index).start()
    for index in (1, 2):
        z_copy(index).start()
    c_copy(0).start()

    turn(own)
    xb[:, rows_sent:deep, :] = jnp.zeros((16, deep - rows_sent, points), bf16)
    acc_a[...] = jnp.zeros_like(acc_a)
    acc_b[...] = jnp.zeros_like(acc_b)
    rest = res_ref[...]
    old = nt(rest, rest, highest)

    def cross(t, into):
        i, k = tile_at(t)
        left = la[pl.ds(pl.multiple_of(i * 512, 512), 512), :]
        into[:, 0:256] = jnp.dot(left, xb[2 * k], preferred_element_type=f32)
        into[:, 256:512] = jnp.dot(left, xb[2 * k + 1], preferred_element_type=f32)

    def consume(t, held):
        i, k = tile_at(t)
        weight = jnp.where((i >= 3) & ((k == 0) | (k == 7)), 0.5, 1.0).astype(f32)
        rows = pl.ds(pl.multiple_of(i * 512, 512), 512)
        values = jnp.exp(held[...] * scale)
        high = values.astype(bf16)
        low = ((values - high.astype(f32)) * low_scale).astype(f8)
        right = jnp.concatenate(
            [xb[2 * k, hi_at:rows_sent, :], xb[2 * k + 1, hi_at:rows_sent, :]], axis=1
        )
        acc_a[rows, 0:32] += nt(high, right) * weight
        acc_a[rows, 32:64] += nt(low, low_parts(right)) * weight
        left = jnp.concatenate(
            [xa[2 * i, hi_at:rows_sent, :], xa[2 * i + 1, hi_at:rows_sent, :]], axis=1
        )
        by_high = jnp.dot(left, high, preferred_element_type=f32) * weight
        by_low = jnp.dot(low_parts(left), low, preferred_element_type=f32) * weight
        for side in (0, 1):
            lanes = slice(side * 256, side * 256 + 256)
            acc_b[2 * k + side, 0:32, :] += by_high[:, lanes]
            acc_b[2 * k + side, 32:64, :] += by_low[:, lanes]

    def b_copy(slot):
        return pltpu.make_async_remote_copy(
            src_ref=part_b.at[slot], dst_ref=sum_b.at[slot],
            send_sem=pb_send.at[slot], recv_sem=pb_recv.at[slot],
            device_id=device(dz=along_z[slot // 2], dc=slot % 2), device_id_type=MESH,
        )

    def hand_back(*which):
        for k in which:
            for slot in (2 * k, 2 * k + 1):
                part_b[slot] = combine(acc_b[slot])
                if slot:
                    b_copy(slot).start()

    def first():
        for index in (0, 1):
            a_copy(index).wait_recv()
        for index in (1, 2):
            z_copy(index).wait_recv()
        for index in (2, 3, 7):
            a_copy(index).start()
        for index in (3, 4):
            z_copy(index).start()
        for slot in (1, 2):
            c_copy(slot).start()
        turn(0)
        turn(1)
        for slot in (0, 1, 2):
            c_copy(slot).wait_recv()

    def second():
        for index in (2, 3, 7):
            a_copy(index).wait_recv()
        for index in (3, 4):
            z_copy(index).wait_recv()
        for index in (4, 5):
            a_copy(index).start()
        for index in (5, 6):
            z_copy(index).start()
        for slot in (3, 4):
            c_copy(slot).start()
        for index in (2, 3, 7):
            turn(index)
        for slot in (3, 4):
            c_copy(slot).wait_recv()

    def third():
        for index in (4, 5):
            a_copy(index).wait_recv()
        for index in (5, 6):
            z_copy(index).wait_recv()
        for index in (6, 9):
            a_copy(index).start()
        for index in (7, 8):
            z_copy(index).start()
        for slot in (5, 6):
            c_copy(slot).start()
        for index in (4, 5):
            turn(index)
        for slot in (5, 6):
            c_copy(slot).wait_recv()

    def fourth():
        for index in (6, 9):
            a_copy(index).wait_recv()
        for index in (7, 8):
            z_copy(index).wait_recv()
        c_copy(7).start()
        for index in (6, 9):
            turn(index)
        c_copy(7).wait_recv()

    events = {1: second, 4: third, 10: fourth}
    ready = {8: (2, 4), 9: (6,), 12: (0,), 13: (1,), 14: (3,), 15: (5,)}
    for at_step, which in ready.items():
        events[at_step] = functools.partial(hand_back, *which)

    first()
    cross(jnp.int32(0), s0)

    def step(n, carry):
        for at_step, act in events.items():
            pl.when(n == at_step)(act)
        t = 2 * n
        cross(t + 1, s1)
        consume(t, s0)
        cross(t + 2, s0)
        consume(t + 1, s1)
        return carry

    lax.fori_loop(0, tiles // 2, step, 0)

    hand_back(7)

    def pa_copy(index):
        (ox, oy), _ = slots[index]
        return pltpu.make_async_remote_copy(
            src_ref=part_a.at[index], dst_ref=sum_a.at[index],
            send_sem=pa_send.at[index], recv_sem=pa_recv.at[index],
            device_id=device(dx=ox, dy=oy), device_id_type=MESH,
        )

    others = [index for index in range(10) if index != own]
    for index in others + [own]:
        part_a[index] = combine(acc_a[pl.ds(index * points, points), :].T)
        if index != own:
            pa_copy(index).start()

    product = part_a[own] + part_b[0] + ridge_weight * way
    for slot in range(1, 16):
        b_copy(slot).wait_recv()
        product = product + sum_b[slot]
    for index in others:
        pa_copy(index).wait_recv()
        product = product + sum_a[index]

    by_product = nt(jnp.concatenate([way, product, rest], axis=0), product, highest)
    of_product = nt(product, jnp.concatenate([way, rest], axis=0), highest)
    gram[0] = jnp.concatenate(
        [
            0.5 * (by_product[0:16] + of_product[:, 0:16]),
            of_product[:, 16:32],
            by_product[16:32],
            old,
            by_product[32:48],
            jnp.zeros((rubrics, 48), f32),
        ],
        axis=1,
    )

    def xy_copy(o):
        dx, dy = plane[o]
        return pltpu.make_async_remote_copy(
            src_ref=gram.at[0], dst_ref=gram_xy.at[o],
            send_sem=g_send.at[o], recv_sem=g_recv.at[o],
            device_id=device(dx=dx, dy=dy), device_id_type=MESH,
        )

    def zc_copy(o):
        dz, dc = column[o]
        return pltpu.make_async_remote_copy(
            src_ref=gram.at[1], dst_ref=gram_zc.at[o],
            send_sem=g_send.at[15 + o], recv_sem=g_recv.at[15 + o],
            device_id=device(dz=dz, dc=dc), device_id_type=MESH,
        )

    for o in range(15):
        xy_copy(o).start()
    total = gram[0]
    for o in range(15):
        xy_copy(o).wait_recv()
        total = total + gram_xy[o]
    gram[1] = total
    for o in range(15):
        zc_copy(o).start()
    for o in range(15):
        zc_copy(o).wait_recv()
        total = total + gram_zc[o]

    curvature, pr, pp = total[:, 0:16], total[:, 16:32], total[:, 32:48]
    rr, rp = total[:, 48:64], total[:, 64:80]
    curvature_inv, rr_inv = inverse(curvature), inverse(rr)
    alpha_t = nn(rr, curvature_inv)
    alpha = nn(curvature_inv, rr)
    residual_next = rest - nn(alpha_t, product)
    res_out[...] = residual_next
    sol_out[...] = sol_ref[...] + nn(alpha_t, way)
    new_gram = rr - nn(alpha_t, pr) + nn(nn(alpha_t, pp) - rp, alpha)
    beta_t = nn(new_gram, rr_inv)
    dir_out[...] = residual_next + nn(beta_t, way)

    for index in others:
        a_copy(index).wait_send()
        pa_copy(index).wait_send()
    for index in range(1, 9):
        z_copy(index).wait_send()
    for slot in range(8):
        c_copy(slot).wait_send()
    for slot in range(1, 16):
        b_copy(slot).wait_send()
    for o in range(15):
        xy_copy(o).wait_send()
        zc_copy(o).wait_send()


def shards(embeddings, solution, residual, direction):
    small = jax.ShapeDtypeStruct((rubrics, points), f32)
    vmem = pl.BlockSpec(memory_space=pltpu.VMEM)
    dma = pltpu.SemaphoreType.DMA
    return pl.pallas_call(
        kernel,
        out_shape=(small, small, small),
        in_specs=[vmem] * 4,
        out_specs=(vmem,) * 3,
        scratch_shapes=[
            pltpu.VMEM((16, deep, points), bf16),
            pltpu.VMEM((10, rows_sent, points), bf16),
            pltpu.VMEM((10 * points, deep), bf16),
            pltpu.VMEM((10 * points, 64), f32),
            pltpu.VMEM((16, 64, points), f32),
            pltpu.VMEM((512, 512), f32),
            pltpu.VMEM((512, 512), f32),
            pltpu.VMEM((10, rubrics, points), f32),
            pltpu.VMEM((16, rubrics, points), f32),
            pltpu.VMEM((10, rubrics, points), f32),
            pltpu.VMEM((16, rubrics, points), f32),
            pltpu.VMEM((2, rubrics, 128), f32),
            pltpu.VMEM((15, rubrics, 128), f32),
            pltpu.VMEM((15, rubrics, 128), f32),
            dma((10,)), dma((10,)), dma((9,)), dma((9,)), dma((8,)), dma((8,)),
            dma((10,)), dma((10,)), dma((16,)), dma((16,)), dma((30,)), dma((30,)),
        ],
        compiler_params=pltpu.CompilerParams(
            collective_id=0, has_side_effects=True, vmem_limit_bytes=48 * 2**20
        ),
        cost_estimate=pl.CostEstimate(
            flops=20_000_000_000, bytes_accessed=1_000_000, transcendentals=9_000_000
        ),
        name="iteration",
    )(embeddings, solution, residual, direction)


def solution(mesh):
    spec = P(None, ("row", "col"))
    return jax.shard_map(
        shards, mesh=mesh, in_specs=(spec,) * 4, out_specs=(spec,) * 3, check_vma=False
    )
```

```python
import functools

import jax
import jax.numpy as jnp
from jax import lax
from jax.experimental import pallas as pl
from jax.experimental.pallas import tpu as pltpu
from jax.sharding import PartitionSpec as P

f32, bf16, f8 = jnp.float32, jnp.bfloat16, jnp.float8_e4m3fn
MESH = pl.DeviceIdType.MESH
highest = lax.Precision.HIGHEST

ridge_weight = 0.5
points = 256
rubrics = 16
width = 384
deep = 512
aug_at, hi_at, lo_at, rows_sent = 384, 400, 416, 432
low_scale, dir_scale, dir_step = 65536.0, 64.0, 16.0
scale = 4.0 / width

slots = [
    ((1, 0), (1, 0)),
    ((0, 3), (0, 3)),
    ((1, 3), (1, 0)),
    ((1, 1), (0, 1)),
    ((2, 1), (1, 0)),
    ((3, 2), (3, 0)),
    ((2, 0), (0, 3)),
    ((2, 2), (0, 1)),
    ((0, 0), None),
    ((0, 2), (0, 3)),
]
own = 8
others = [index for index in range(10) if index != own]
place = {offset: index for index, (offset, _) in enumerate(slots)}
along_z = [0, 1, 7, 2, 6, 3, 5, 4]
half_rows = 208
runs = [
    (3, 0, 0, 0, 1),
    (3, 1, 0, 0, 1),
    (2, 0, 0, 3, 1),
    (2, 1, 0, 3, 1),
    (1, 4, 0, 3, 0),
    (5, 2, 0, 0, 1),
    (3, 0, 1, 6, 0),
    (3, 0, 1, 5, 0),
    (5, 0, 1, 7, 0),
    (3, 3, 0, 5, -2),
    (1, 3, 0, 0, 0),
    (2, 4, 0, 5, -4),
    (1, 4, 0, 0, 0),
]
tiles = 34


def parent(index):
    (ox, oy), (hx, hy) = slots[index]
    return place[((ox - hx) % 4, (oy - hy) % 4)]


def tile_at(t):
    i, k, start = 0, 0, 0
    for count, i0, i_step, k0, k_step in runs:
        late = t - start
        i = jnp.where(late >= 0, i0 + late * i_step, i)
        k = jnp.where(late >= 0, k0 + late * k_step, k)
        start += count
    beyond = t >= start
    return jnp.where(beyond, 0, i), jnp.where(beyond, 0, k)


def nt(left, right, precision=None):
    return lax.dot_general(
        left, right, (((1,), (1,)), ((), ())), precision=precision, preferred_element_type=f32
    )


def nn(left, right):
    return jnp.dot(left, right, precision=highest, preferred_element_type=f32)


def low_parts(pieces):
    whole = pieces.astype(f32)
    whole = (whole[:rubrics] + whole[rubrics:]) * dir_scale
    first = whole.astype(f8)
    second = ((whole - first.astype(f32)) * dir_step).astype(f8)
    return jnp.concatenate([first, second], axis=0)


def combine(parts):
    low = parts[32:48] + parts[48:64] * (1.0 / dir_step)
    return parts[0:16] + parts[16:32] + low * (1.0 / (low_scale * dir_scale))


def pack(matrix):
    return jnp.concatenate([matrix[0:8], matrix[8:16]], axis=1)


def unpack(packed, at):
    return jnp.concatenate([packed[:, at : at + 16], packed[:, at + 16 : at + 32]], axis=0)


def inverse(matrix):
    size = matrix.shape[0]
    row = lax.broadcasted_iota(jnp.int32, matrix.shape, 0)
    col = lax.broadcasted_iota(jnp.int32, matrix.shape, 1)
    for step in range(size):
        pivot_row = matrix[step : step + 1, :]
        pivot_col = matrix[:, step : step + 1]
        pivot = 1.0 / matrix[step : step + 1, step : step + 1]
        scaled = pivot_row * pivot
        inner = matrix - pivot_col * scaled
        at_row, at_col = row == step, col == step
        matrix = jnp.where(
            at_row,
            jnp.where(at_col, pivot, scaled),
            jnp.where(at_col, -pivot_col * pivot, inner),
        )
    return matrix


def kernel(
    e_hbm, sol_hbm, res_hbm, dir_hbm, sol_out, res_out, dir_out,
    e_ref, sol_ref, res_ref, dir_ref,
    xb, xa, la, acc_a, acc_b, s0, s1, part_a, part_b, sum_a, sum_b, gram, gram_in, old, old_in,
    in_sem, a_send, a_recv, z_send, z_recv, c_send, c_recv, pa_send, pa_recv, pb_send, pb_recv,
    g_send, g_recv, o_send, o_recv,
):
    row, col = lax.axis_index("row"), lax.axis_index("col")
    core, x, z_lo = lax.rem(row, 2), lax.rem(lax.div(row, 2), 4), lax.div(row, 8)
    y, z_hi = lax.div(col, 4), lax.rem(col, 4)
    z = z_hi * 2 + z_lo

    def device(dx=0, dy=0, dz=0, dc=0):
        x2, y2 = lax.rem(x + dx % 4, 4), lax.rem(y + dy % 4, 4)
        z2, c2 = lax.rem(z + dz % 8, 8), lax.rem(core + dc, 2)
        return (lax.rem(z2, 2) * 8 + x2 * 2 + c2, y2 * 4 + lax.div(z2, 2))

    fetch = [
        pltpu.make_async_copy(source, into, in_sem.at[n])
        for n, (source, into) in enumerate(
            ((e_hbm, e_ref), (dir_hbm, dir_ref), (res_hbm, res_ref), (sol_hbm, sol_ref))
        )
    ]
    for copy in fetch:
        copy.start()
    barrier = pltpu.get_barrier_semaphore()
    neighbours = [
        device(dx=1), device(dx=3), device(dy=1), device(dy=3), device(dz=1), device(dz=7), device(dc=1)
    ]
    for neighbour in neighbours:
        pl.semaphore_signal(barrier, inc=1, device_id=neighbour, device_id_type=MESH)

    fetch[0].wait()
    fetch[1].wait()
    block = e_ref[...]
    wide = block.astype(f32)
    half = -0.5 * jnp.sum(wide * wide, axis=0, keepdims=True)
    h1 = half.astype(bf16).astype(f32)
    h2 = (half - h1).astype(bf16).astype(f32)
    h3 = half - h1 - h2
    at = lax.broadcasted_iota(jnp.int32, (16, points), 0)
    ones = jnp.where((at >= 8) & (at < 11), 1.0, 0.0)
    aug = jnp.where(at == 0, h1, jnp.where(at == 1, h2, jnp.where(at == 2, h3, ones)))
    way = dir_ref[...]
    way_hi = way.astype(bf16)
    way_lo = (way - way_hi.astype(f32)).astype(bf16)
    for buffer, slot in ((xb, 0), (xa, own)):
        buffer[slot, 0:width, :] = block
        buffer[slot, aug_at:hi_at, :] = aug.astype(bf16)
        buffer[slot, hi_at:lo_at, :] = way_hi
        buffer[slot, lo_at:rows_sent, :] = way_lo

    pl.semaphore_wait(barrier, len(neighbours))

    body_rows = pl.ds(0, rows_sent)

    def remote(source, target, send, recv, to):
        return pltpu.make_async_remote_copy(
            src_ref=source, dst_ref=target, send_sem=send, recv_sem=recv,
            device_id=to, device_id_type=MESH,
        )

    def a_copy(index):
        hx, hy = slots[index][1]
        return remote(
            xa.at[parent(index)], xa.at[index], a_send.at[index], a_recv.at[index], device(dx=-hx, dy=-hy)
        )

    def z_copy(index):
        slot = min(index, 7)
        source = [None, 0, 0, 1, 2, 3, 4, 5, 6][index]
        rows = body_rows
        if index == 7:
            rows = pl.ds(0, half_rows)
        if index == 8:
            rows = pl.ds(half_rows, rows_sent - half_rows)
        step = -1 if index in (1, 3, 5, 7) else 1
        return remote(
            xb.at[2 * source, rows, :], xb.at[2 * slot, rows, :], z_send.at[index], z_recv.at[index],
            device(dz=step),
        )

    def c_copy(slot):
        return remote(
            xb.at[2 * slot, body_rows, :], xb.at[2 * slot + 1, body_rows, :], c_send.at[slot], c_recv.at[slot],
            device(dc=1),
        )

    def turn(index):
        rows = pl.ds(index * points, points)
        la[rows, 0:width] = xa[index, 0:width, :].T
        extra = xa[index, aug_at:hi_at, :].astype(f32)
        extra = jnp.concatenate([extra[8:16], extra[0:8], jnp.zeros((112, points), f32)], axis=0)
        la[rows, width:deep] = extra.T.astype(bf16)

    for index in (0, 1):
        a_copy(index).start()
    for index in (1, 2):
        z_copy(index).start()
    c_copy(0).start()

    turn(own)
    xb[:, rows_sent:deep, :] = jnp.zeros((16, deep - rows_sent, points), bf16)
    acc_a[...] = jnp.zeros_like(acc_a)
    acc_b[...] = jnp.zeros_like(acc_b)
    fetch[2].wait()
    fetch[3].wait()
    rest = res_ref[...]
    empty = jnp.zeros((8, 96), f32)
    old[0] = jnp.concatenate([pack(nt(rest, rest, highest)), empty], axis=1)

    def cross(t, into):
        i, k = tile_at(t)
        left = la[pl.ds(pl.multiple_of(i * 512, 512), 512), :]
        into[:, 0:256] = jnp.dot(left, xb[2 * k], preferred_element_type=f32)
        into[:, 256:512] = jnp.dot(left, xb[2 * k + 1], preferred_element_type=f32)

    def consume(t, held):
        i, k = tile_at(t)
        weight = jnp.where((i >= 3) & ((k == 0) | (k == 7)), 0.5, 1.0).astype(f32)
        rows = pl.ds(pl.multiple_of(i * 512, 512), 512)
        values = jnp.exp(held[...] * scale)
        high = values.astype(bf16)
        low = ((values - high.astype(f32)) * low_scale).astype(f8)
        right = jnp.concatenate(
            [xb[2 * k, hi_at:rows_sent, :], xb[2 * k + 1, hi_at:rows_sent, :]], axis=1
        )
        acc_a[rows, 0:32] += nt(high, right) * weight
        acc_a[rows, 32:64] += nt(low, low_parts(right)) * weight
        left = jnp.concatenate(
            [xa[2 * i, hi_at:rows_sent, :], xa[2 * i + 1, hi_at:rows_sent, :]], axis=1
        )
        by_high = jnp.dot(left, high, preferred_element_type=f32) * weight
        by_low = jnp.dot(low_parts(left), low, preferred_element_type=f32) * weight
        for side in (0, 1):
            lanes = slice(side * 256, side * 256 + 256)
            acc_b[2 * k + side, 0:32, :] += by_high[:, lanes]
            acc_b[2 * k + side, 32:64, :] += by_low[:, lanes]

    def b_copy(slot):
        return remote(
            part_b.at[slot], sum_b.at[slot], pb_send.at[slot], pb_recv.at[slot],
            device(dz=along_z[slot // 2], dc=slot % 2),
        )

    def hand_b(*which):
        for k in which:
            for slot in (2 * k, 2 * k + 1):
                part_b[slot] = combine(acc_b[slot])
                if slot:
                    b_copy(slot).start()

    def pa_copy(index):
        ox, oy = slots[index][0]
        return remote(
            part_a.at[index], sum_a.at[index], pa_send.at[index], pa_recv.at[index], device(dx=ox, dy=oy)
        )

    def hand_a(*which):
        for index in which:
            part_a[index] = combine(acc_a[pl.ds(index * points, points), :].T)
            if index != own:
                pa_copy(index).start()

    def sum_copies(sent, landed, send, recv):
        copies = []
        for n in range(30):
            o = n % 15 + 1
            to = device(dx=o // 4, dy=o % 4) if n < 15 else device(dz=o // 2, dc=o % 2)
            copies.append(remote(sent.at[n // 15], landed.at[n], send.at[n], recv.at[n], to))
        return copies

    def start_stage(copies, stage):
        for copy in copies[15 * stage : 15 * stage + 15]:
            copy.start()

    def finish_stage(copies, sent, landed, stage):
        total = sent[stage]
        for n in range(15 * stage, 15 * stage + 15):
            copies[n].wait_recv()
            total = total + landed[n]
        return total

    old_copies = sum_copies(old, old_in, o_send, o_recv)
    gram_copies = sum_copies(gram, gram_in, g_send, g_recv)

    def first():
        for index in (0, 1):
            a_copy(index).wait_recv()
        for index in (1, 2):
            z_copy(index).wait_recv()
        for slot in (1, 2):
            c_copy(slot).start()
        for index in (9, 2, 3):
            a_copy(index).start()
        for index in (3, 4):
            z_copy(index).start()
        turn(0)
        turn(1)
        c_copy(0).wait_recv()

    def second():
        for index in (2, 3, 9):
            a_copy(index).wait_recv()
        for index in (3, 4):
            z_copy(index).wait_recv()
        for slot in (3, 4):
            c_copy(slot).start()
        for index in (4, 5):
            a_copy(index).start()
        for index in (5, 6):
            z_copy(index).start()
        for index in (2, 3, 9):
            turn(index)

    def third():
        for index in (4, 5):
            a_copy(index).wait_recv()
        for index in (5, 6):
            z_copy(index).wait_recv()
        for slot in (5, 6):
            c_copy(slot).start()
        for index in (6, 7):
            a_copy(index).start()
        for index in (7, 8):
            z_copy(index).start()
        for index in (4, 5):
            turn(index)

    def fourth():
        for index in (7, 8):
            z_copy(index).wait_recv()
        c_copy(7).start()
        for index in (6, 7):
            a_copy(index).wait_recv()
        for index in (6, 7):
            turn(index)

    def siblings(*which):
        for slot in which:
            c_copy(slot).wait_recv()

    def old_first():
        start_stage(old_copies, 0)

    def old_second():
        old[1] = finish_stage(old_copies, old, old_in, 0)
        start_stage(old_copies, 1)

    def old_third():
        old[2] = finish_stage(old_copies, old, old_in, 1)

    bind = functools.partial
    events = {
        0: [bind(siblings, 1, 2)],
        1: [second],
        2: [bind(siblings, 3, 4)],
        5: [third],
        7: [bind(siblings, 5, 6), bind(hand_b, 2)],
        8: [bind(hand_b, 4), old_first],
        9: [fourth],
        10: [bind(siblings, 7), bind(hand_b, 6)],
        11: [old_second],
        13: [bind(hand_a, 0, 1, 2, 3, 4, 5)],
        14: [bind(hand_b, 7), old_third],
        15: [bind(hand_b, 3)],
        16: [bind(hand_a, 6, 7), bind(hand_b, 5)],
    }

    first()
    cross(jnp.int32(0), s0)

    def step(n, carry):
        for at_step, acts in events.items():

            @pl.when(n == at_step)
            def _(acts=acts):
                for act in acts:
                    act()

        t = 2 * n
        cross(t + 1, s1)
        consume(t, s0)
        cross(t + 2, s0)
        consume(t + 1, s1)
        return carry

    lax.fori_loop(0, tiles // 2, step, 0)

    hand_a(9)
    hand_b(1, 0)
    hand_a(own)
    rr = unpack(old[2], 0)
    rr_inv = inverse(rr)
    product = part_a[own] + part_b[0] + ridge_weight * way
    for slot in (4, 5, 8, 9, 12, 13, 14, 15, 6, 7, 10, 11):
        b_copy(slot).wait_recv()
        product = product + sum_b[slot]
    for index in (0, 1, 2, 3, 4, 5, 6, 7, 9):
        pa_copy(index).wait_recv()
        product = product + sum_a[index]
    for slot in (1, 2, 3):
        b_copy(slot).wait_recv()
        product = product + sum_b[slot]

    by_product = nt(jnp.concatenate([way, product], axis=0), product, highest)
    of_product = nt(product, jnp.concatenate([way, rest], axis=0), highest)
    curvature = 0.5 * (by_product[0:16] + of_product[:, 0:16])
    gram[0] = jnp.concatenate(
        [pack(curvature), pack(of_product[:, 16:32]), pack(by_product[16:32]), empty[:, 0:32]], axis=1
    )
    start_stage(gram_copies, 0)
    gram[1] = finish_stage(gram_copies, gram, gram_in, 0)
    start_stage(gram_copies, 1)
    total = finish_stage(gram_copies, gram, gram_in, 1)

    curvature, pr, pp = unpack(total, 0), unpack(total, 32), unpack(total, 64)
    curvature_inv = inverse(curvature)
    alpha_t = nn(rr, curvature_inv)
    alpha = nn(curvature_inv, rr)
    residual_next = rest - nn(alpha_t, product)
    res_out[...] = residual_next
    sol_out[...] = sol_ref[...] + nn(alpha_t, way)
    crossed = nn(alpha_t, pr)
    new_gram = rr - crossed - crossed.T + nn(nn(alpha_t, pp), alpha)
    beta_t = nn(new_gram, rr_inv)
    dir_out[...] = residual_next + nn(beta_t, way)

    for index in others:
        a_copy(index).wait_send()
        pa_copy(index).wait_send()
    for index in range(1, 9):
        z_copy(index).wait_send()
    for slot in range(8):
        c_copy(slot).wait_send()
    for slot in range(1, 16):
        b_copy(slot).wait_send()
    for copy in old_copies + gram_copies:
        copy.wait_send()


def shards(embeddings, solution, residual, direction):
    small = jax.ShapeDtypeStruct((rubrics, points), f32)
    vmem = pl.BlockSpec(memory_space=pltpu.VMEM)
    dma = pltpu.SemaphoreType.DMA
    return pl.pallas_call(
        kernel,
        out_shape=(small, small, small),
        in_specs=[pl.BlockSpec(memory_space=pl.ANY)] * 4,
        out_specs=(vmem,) * 3,
        scratch_shapes=[
            pltpu.VMEM((width, points), bf16),
            pltpu.VMEM((rubrics, points), f32),
            pltpu.VMEM((rubrics, points), f32),
            pltpu.VMEM((rubrics, points), f32),
            pltpu.VMEM((16, deep, points), bf16),
            pltpu.VMEM((10, rows_sent, points), bf16),
            pltpu.VMEM((10 * points, deep), bf16),
            pltpu.VMEM((10 * points, 64), f32),
            pltpu.VMEM((16, 64, points), f32),
            pltpu.VMEM((512, 512), f32),
            pltpu.VMEM((512, 512), f32),
            pltpu.VMEM((10, rubrics, points), f32),
            pltpu.VMEM((16, rubrics, points), f32),
            pltpu.VMEM((10, rubrics, points), f32),
            pltpu.VMEM((16, rubrics, points), f32),
            pltpu.VMEM((2, 8, 128), f32),
            pltpu.VMEM((30, 8, 128), f32),
            pltpu.VMEM((3, 8, 128), f32),
            pltpu.VMEM((30, 8, 128), f32),
            dma((4,)), dma((10,)), dma((10,)), dma((9,)), dma((9,)), dma((8,)), dma((8,)),
            dma((10,)), dma((10,)), dma((16,)), dma((16,)), dma((30,)), dma((30,)), dma((30,)), dma((30,)),
        ],
        compiler_params=pltpu.CompilerParams(
            collective_id=0, has_side_effects=True, vmem_limit_bytes=56 * 2**20
        ),
        cost_estimate=pl.CostEstimate(
            flops=20_000_000_000, bytes_accessed=1_000_000, transcendentals=9_000_000
        ),
        name="iteration",
    )(embeddings, solution, residual, direction)


def solution(mesh):
    spec = P(None, ("row", "col"))
    return jax.shard_map(
        shards, mesh=mesh, in_specs=(spec,) * 4, out_specs=(spec,) * 3, check_vma=False
    )
```

```python
import functools

import jax
import jax.numpy as jnp
from jax import lax
from jax.experimental import pallas as pl
from jax.experimental.pallas import tpu as pltpu
from jax.sharding import PartitionSpec as P

f32, bf16, f8 = jnp.float32, jnp.bfloat16, jnp.float8_e4m3fn
MESH = pl.DeviceIdType.MESH
highest = lax.Precision.HIGHEST

ridge_weight = 0.5
points = 256
rubrics = 16
width = 384
deep = 512
aug_at, hi_at, lo_at, rows_sent = 384, 400, 416, 432
low_scale, dir_scale, dir_step = 65536.0, 64.0, 16.0
scale = 4.0 / width

slots = [
    ((1, 0), (1, 0)),
    ((0, 3), (0, 3)),
    ((1, 3), (1, 0)),
    ((1, 1), (0, 1)),
    ((2, 1), (1, 0)),
    ((3, 2), (3, 0)),
    ((2, 0), (0, 3)),
    ((2, 2), (0, 1)),
    ((0, 0), None),
    ((0, 2), (0, 3)),
]
own = 8
others = [index for index in range(10) if index != own]
place = {offset: index for index, (offset, _) in enumerate(slots)}
along_z = [0, 1, 7, 2, 6, 3, 5, 4]
half_rows = 208
opening = [(0, 0), (0, 1), (0, 2)]
main = [
    [(1, 0), (1, 1), (1, 2), (4, 1)],
    [(0, 3), (0, 4), (1, 3), (1, 4)],
    [(2, 0), (2, 1), (2, 2), (2, 3)],
    [(2, 4), (0, 6), (1, 6), (2, 6)],
    [(0, 5), (1, 5), (2, 5), (4, 5)],
    [(3, 5), (3, 3), (3, 1), (3, "both")],
    [(0, 7), (1, 7), (2, 7), (4, 7)],
]
closing = [(4, 3), (4, 0)]


def parent(index):
    (ox, oy), (hx, hy) = slots[index]
    return place[((ox - hx) % 4, (oy - hy) % 4)]


def pick(n, values):
    value = values[0]
    for index in range(1, len(values)):
        if values[index] != values[index - 1]:
            value = jnp.where(n >= index, values[index], value)
    return value


def nt(left, right, precision=None):
    return lax.dot_general(
        left, right, (((1,), (1,)), ((), ())), precision=precision, preferred_element_type=f32
    )


def nn(left, right):
    return jnp.dot(left, right, precision=highest, preferred_element_type=f32)


def low_parts(pieces):
    whole = pieces.astype(f32)
    whole = (whole[:rubrics] + whole[rubrics:]) * dir_scale
    first = whole.astype(f8)
    second = ((whole - first.astype(f32)) * dir_step).astype(f8)
    return jnp.concatenate([first, second], axis=0)


def combine(parts):
    low = parts[32:48] + parts[48:64] * (1.0 / dir_step)
    return parts[0:16] + parts[16:32] + low * (1.0 / (low_scale * dir_scale))


def pack(matrix):
    return jnp.concatenate([matrix[0:8], matrix[8:16]], axis=1)


def unpack(packed, at):
    return jnp.concatenate([packed[:, at : at + 16], packed[:, at + 16 : at + 32]], axis=0)


def inverse(matrix):
    row = lax.broadcasted_iota(jnp.int32, matrix.shape, 0)
    col = lax.broadcasted_iota(jnp.int32, matrix.shape, 1)
    for s in range(0, matrix.shape[0], 2):
        e = s + 1
        one, two = matrix[s:e, :], matrix[e : e + 1, :]
        col_one, col_two = matrix[:, s:e], matrix[:, e : e + 1]
        a, b, c, d = one[:, s:e], one[:, e : e + 1], two[:, s:e], two[:, e : e + 1]
        share = 1.0 / (a * d - b * c)
        first, second = col == s, col == e
        one = jnp.where(first[0:1], 1.0, jnp.where(second[0:1], 0.0, one))
        two = jnp.where(first[0:1], 0.0, jnp.where(second[0:1], 1.0, two))
        new_one = (d * share) * one - (b * share) * two
        new_two = (a * share) * two - (c * share) * one
        inner = jnp.where(first | second, 0.0, matrix) - col_one * new_one - col_two * new_two
        matrix = jnp.where(row == s, new_one, jnp.where(row == e, new_two, inner))
    return matrix


def kernel(
    e_hbm, sol_hbm, res_hbm, dir_hbm, out,
    e_ref, sol_ref, res_ref, dir_ref,
    xb, xa, la, acc_a, acc_b, part_a, part_b, sum_a, sum_b, gram, gram_in, old, old_in,
    in_sem, a_send, a_recv, z_send, z_recv, c_send, c_recv, pa_send, pa_recv, pb_send, pb_recv,
    g_send, g_recv, o_send, o_recv,
):
    row, col = lax.axis_index("row"), lax.axis_index("col")
    core, x, z_lo = lax.rem(row, 2), lax.rem(lax.div(row, 2), 4), lax.div(row, 8)
    y, z_hi = lax.div(col, 4), lax.rem(col, 4)
    z = z_hi * 2 + z_lo

    def device(dx=0, dy=0, dz=0, dc=0):
        x2, y2 = lax.rem(x + dx % 4, 4), lax.rem(y + dy % 4, 4)
        z2, c2 = lax.rem(z + dz % 8, 8), lax.rem(core + dc, 2)
        return (lax.rem(z2, 2) * 8 + x2 * 2 + c2, y2 * 4 + lax.div(z2, 2))

    fetch = [
        pltpu.make_async_copy(source, into, in_sem.at[n])
        for n, (source, into) in enumerate(
            ((e_hbm, e_ref), (dir_hbm, dir_ref), (res_hbm, res_ref), (sol_hbm, sol_ref))
        )
    ]
    for copy in fetch:
        copy.start()
    barrier = pltpu.get_barrier_semaphore()
    neighbours = [
        device(dx=1), device(dx=3), device(dy=1), device(dy=3), device(dz=1), device(dz=7), device(dc=1)
    ]
    for neighbour in neighbours:
        pl.semaphore_signal(barrier, inc=1, device_id=neighbour, device_id_type=MESH)

    fetch[0].wait()
    fetch[1].wait()
    block = e_ref[...]
    wide = block.astype(f32)
    half = -0.5 * jnp.sum(wide * wide, axis=0, keepdims=True)
    h1 = half.astype(bf16).astype(f32)
    h2 = (half - h1).astype(bf16).astype(f32)
    h3 = half - h1 - h2
    at = lax.broadcasted_iota(jnp.int32, (16, points), 0)
    ones = jnp.where((at >= 8) & (at < 11), 1.0, 0.0)
    aug = jnp.where(at == 0, h1, jnp.where(at == 1, h2, jnp.where(at == 2, h3, ones)))
    way = dir_ref[...]
    way_hi = way.astype(bf16)
    way_lo = (way - way_hi.astype(f32)).astype(bf16)
    for buffer, slot in ((xb, 0), (xa, own)):
        buffer[slot, 0:width, :] = block
        buffer[slot, aug_at:hi_at, :] = aug.astype(bf16)
        buffer[slot, hi_at:lo_at, :] = way_hi
        buffer[slot, lo_at:rows_sent, :] = way_lo

    pl.semaphore_wait(barrier, len(neighbours))

    body_rows = pl.ds(0, rows_sent)

    def remote(source, target, send, recv, to):
        return pltpu.make_async_remote_copy(
            src_ref=source, dst_ref=target, send_sem=send, recv_sem=recv,
            device_id=to, device_id_type=MESH,
        )

    def a_copy(index):
        hx, hy = slots[index][1]
        return remote(
            xa.at[parent(index)], xa.at[index], a_send.at[index], a_recv.at[index], device(dx=-hx, dy=-hy)
        )

    def z_copy(index):
        slot = min(index, 7)
        source = [None, 0, 0, 1, 2, 3, 4, 5, 6][index]
        rows = body_rows
        if index == 7:
            rows = pl.ds(0, half_rows)
        if index == 8:
            rows = pl.ds(half_rows, rows_sent - half_rows)
        step = -1 if index in (1, 3, 5, 7) else 1
        return remote(
            xb.at[2 * source, rows, :], xb.at[2 * slot, rows, :], z_send.at[index], z_recv.at[index],
            device(dz=step),
        )

    def c_copy(slot):
        return remote(
            xb.at[2 * slot, body_rows, :], xb.at[2 * slot + 1, body_rows, :], c_send.at[slot], c_recv.at[slot],
            device(dc=1),
        )

    def turn(index):
        rows = pl.ds(index * points, points)
        la[rows, 0:width] = xa[index, 0:width, :].T
        extra = xa[index, aug_at:hi_at, :].astype(f32)
        extra = jnp.concatenate([extra[8:16], extra[0:8], jnp.zeros((112, points), f32)], axis=0)
        la[rows, width:deep] = extra.T.astype(bf16)

    for index in (0, 1):
        a_copy(index).start()
    for index in (1, 2):
        z_copy(index).start()
    c_copy(0).start()

    turn(own)
    xb[:, rows_sent:deep, :] = jnp.zeros((16, deep - rows_sent, points), bf16)
    acc_a[...] = jnp.zeros_like(acc_a)
    acc_b[...] = jnp.zeros_like(acc_b)
    fetch[2].wait()
    fetch[3].wait()
    rest = res_ref[...]
    empty = jnp.zeros((8, 96), f32)
    old[0] = jnp.concatenate([pack(nt(rest, rest, highest)), empty], axis=1)

    def tile(i, one, two, weight):
        rows = pl.ds(pl.multiple_of(i * 512, 512), 512)
        lhs = la[rows, :]
        halves = [jnp.dot(lhs, xb[slot], preferred_element_type=f32) for slot in (one, two)]
        values = jnp.exp(jnp.concatenate(halves, axis=1) * scale)
        high = values.astype(bf16)
        low = ((values - high.astype(f32)) * low_scale).astype(f8)
        right = jnp.concatenate(
            [xb[one, hi_at:rows_sent, :], xb[two, hi_at:rows_sent, :]], axis=1
        )
        acc_a[rows, 0:32] += nt(high, right) * weight
        acc_a[rows, 32:64] += nt(low, low_parts(right)) * weight
        left = jnp.concatenate(
            [xa[2 * i, hi_at:rows_sent, :], xa[2 * i + 1, hi_at:rows_sent, :]], axis=1
        )
        by_high = jnp.dot(left, high, preferred_element_type=f32) * weight
        by_low = jnp.dot(low_parts(left), low, preferred_element_type=f32) * weight
        for slot, lanes in ((one, slice(0, 256)), (two, slice(256, 512))):
            acc_b[slot, 0:32, :] += by_high[:, lanes]
            acc_b[slot, 32:64, :] += by_low[:, lanes]

    mine = jnp.where(x < 2, 0, 1)

    def run_tile(i, k):
        tile(i, 2 * k, 2 * k + 1, 0.5 if i == 4 and k in (0, 7) else 1.0)

    def run_tiles(n, groups):
        i = pick(n, [i for i, _ in groups])
        at_one = pick(n, [0 if k == "both" else 2 * k for _, k in groups])
        at_two = pick(n, [14 if k == "both" else 2 * k + 1 for _, k in groups])
        weight = pick(n, [0.5 if i == 4 and k in (0, 7) else 1.0 for i, k in groups])
        if any(k == "both" for _, k in groups):
            shift = pick(n, [1 if k == "both" else 0 for _, k in groups]) * mine
            at_one, at_two = at_one + shift, at_two + shift
        tile(i, at_one, at_two, weight)

    def b_copy(slot):
        return remote(
            part_b.at[slot], sum_b.at[slot], pb_send.at[slot], pb_recv.at[slot],
            device(dz=along_z[slot // 2], dc=slot % 2),
        )

    def hand_b(*which):
        for k in which:
            for slot in (2 * k, 2 * k + 1):
                part_b[slot] = combine(acc_b[slot])
                if slot:
                    b_copy(slot).start()

    def pa_copy(index):
        ox, oy = slots[index][0]
        return remote(
            part_a.at[index], sum_a.at[index], pa_send.at[index], pa_recv.at[index], device(dx=ox, dy=oy)
        )

    def hand_a(*which):
        for index in which:
            part_a[index] = combine(acc_a[pl.ds(index * points, points), :].T)
            if index != own:
                pa_copy(index).start()

    def sum_copies(sent, landed, send, recv):
        plane = sorted(range(1, 16), key=lambda o: -min(o // 4, 4 - o // 4) - min(o % 4, 4 - o % 4))
        column = sorted(range(1, 16), key=lambda o: -min(o // 2, 8 - o // 2))
        targets = [device(dx=o // 4, dy=o % 4) for o in plane]
        targets += [device(dz=o // 2, dc=o % 2) for o in column]
        return [
            remote(sent.at[n // 15], landed.at[n], send.at[n], recv.at[n], to) for n, to in enumerate(targets)
        ]

    def start_stage(copies, stage):
        for copy in copies[15 * stage : 15 * stage + 15]:
            copy.start()

    def finish_stage(copies, sent, landed, stage):
        total = sent[stage]
        for n in range(15 * stage, 15 * stage + 15):
            copies[n].wait_recv()
            total = total + landed[n]
        return total

    old_copies = sum_copies(old, old_in, o_send, o_recv)
    gram_copies = sum_copies(gram, gram_in, g_send, g_recv)

    def first():
        for index in (0, 1):
            a_copy(index).wait_recv()
        for index in (1, 2):
            z_copy(index).wait_recv()
        for slot in (1, 2):
            c_copy(slot).start()
        for index in (9, 2, 3):
            a_copy(index).start()
        for index in (3, 4):
            z_copy(index).start()
        turn(0)
        turn(1)
        c_copy(0).wait_recv()

    def second():
        for index in (2, 3, 9):
            a_copy(index).wait_recv()
        for index in (3, 4):
            z_copy(index).wait_recv()
        for slot in (3, 4):
            c_copy(slot).start()
        for index in (4, 5):
            a_copy(index).start()
        for index in (5, 6):
            z_copy(index).start()
        for index in (2, 3, 9):
            turn(index)

    def third():
        for index in (4, 5):
            a_copy(index).wait_recv()
        for index in (5, 6):
            z_copy(index).wait_recv()
        for slot in (5, 6):
            c_copy(slot).start()
        for index in (6, 7):
            a_copy(index).start()
        for index in (7, 8):
            z_copy(index).start()
        for index in (4, 5):
            turn(index)

    def fourth():
        for index in (7, 8):
            z_copy(index).wait_recv()
        c_copy(7).start()
        for index in (6, 7):
            a_copy(index).wait_recv()
        for index in (6, 7):
            turn(index)

    def siblings(*which):
        for slot in which:
            c_copy(slot).wait_recv()

    def old_first():
        start_stage(old_copies, 0)

    def old_second():
        old[1] = finish_stage(old_copies, old, old_in, 0)
        start_stage(old_copies, 1)

    bind = functools.partial
    first()

    def open_step(n, carry):
        for slot in (1, 2):
            pl.when(n == slot)(bind(siblings, slot))
        run_tiles(n, opening)
        return carry

    lax.fori_loop(0, len(opening), open_step, 0)

    events = {
        0: [second],
        1: [bind(siblings, 3, 4)],
        2: [third],
        3: [bind(siblings, 5, 6), bind(hand_b, 2), old_first],
        4: [fourth, bind(hand_b, 4, 6)],
        5: [bind(siblings, 7), old_second],
        6: [bind(hand_a, 6, 7), bind(hand_b, 5, 1)],
    }

    def step(n, carry):
        for at_step, acts in events.items():

            @pl.when(n == at_step)
            def _(acts=acts):
                for act in acts:
                    act()

        for u in range(4):
            run_tiles(n, [group[u] for group in main])
        return carry

    lax.fori_loop(0, len(main), step, 0)

    hand_b(7)
    hand_a(4, 5, 2, 3, 0, 1)
    run_tile(*closing[0])
    hand_b(3)
    run_tile(*closing[1])
    hand_a(9)
    hand_b(0)
    hand_a(own)
    rr = unpack(finish_stage(old_copies, old, old_in, 1), 0)
    rr_inv = inverse(rr)
    product = part_a[own] + part_b[0] + ridge_weight * way
    for slot in (4, 5, 8, 9, 12, 13, 10, 11, 2, 3, 14, 15):
        b_copy(slot).wait_recv()
        product = product + sum_b[slot]
    for index in (0, 1, 2, 3, 4, 5, 6, 7, 9):
        pa_copy(index).wait_recv()
        product = product + sum_a[index]
    for slot in (6, 7, 1):
        b_copy(slot).wait_recv()
        product = product + sum_b[slot]

    by_product = nt(jnp.concatenate([way, product], axis=0), product, highest)
    of_product = nt(product, jnp.concatenate([way, rest], axis=0), highest)
    curvature = 0.5 * (by_product[0:16] + of_product[:, 0:16])
    gram[0] = jnp.concatenate(
        [pack(curvature), pack(of_product[:, 16:32]), pack(by_product[16:32]), empty[:, 0:32]], axis=1
    )
    start_stage(gram_copies, 0)
    gram[1] = finish_stage(gram_copies, gram, gram_in, 0)
    start_stage(gram_copies, 1)
    total = finish_stage(gram_copies, gram, gram_in, 1)

    curvature, pr, pp = unpack(total, 0), unpack(total, 32), unpack(total, 64)
    residual_part = nn(pr, rr_inv)
    stacked = jnp.concatenate([rr, pp, pr.T], axis=0)
    by_curvature = nn(stacked, inverse(curvature))
    alpha_t, pp_part, rp_part = by_curvature[0:16], by_curvature[16:32], by_curvature[32:48]
    changed = nn(alpha_t, pp_part - residual_part)
    residual_next = rest - nn(alpha_t, product)
    out[16:32] = residual_next
    out[0:16] = sol_ref[...] + nn(alpha_t, way)
    out[32:48] = residual_next + way + nn(changed - rp_part, way)

    for index in others:
        a_copy(index).wait_send()
        pa_copy(index).wait_send()
    for index in range(1, 9):
        z_copy(index).wait_send()
    for slot in range(8):
        c_copy(slot).wait_send()
    for slot in range(1, 16):
        b_copy(slot).wait_send()
    for copy in old_copies + gram_copies:
        copy.wait_send()


def shards(embeddings, solution, residual, direction):
    vmem = pl.BlockSpec(memory_space=pltpu.VMEM)
    dma = pltpu.SemaphoreType.DMA
    stacked = pl.pallas_call(
        kernel,
        out_shape=jax.ShapeDtypeStruct((3 * rubrics, points), f32),
        in_specs=[pl.BlockSpec(memory_space=pl.ANY)] * 4,
        out_specs=vmem,
        scratch_shapes=[
            pltpu.VMEM((width, points), bf16),
            pltpu.VMEM((rubrics, points), f32),
            pltpu.VMEM((rubrics, points), f32),
            pltpu.VMEM((rubrics, points), f32),
            pltpu.VMEM((16, deep, points), bf16),
            pltpu.VMEM((10, rows_sent, points), bf16),
            pltpu.VMEM((10 * points, deep), bf16),
            pltpu.VMEM((10 * points, 64), f32),
            pltpu.VMEM((16, 64, points), f32),
            pltpu.VMEM((10, rubrics, points), f32),
            pltpu.VMEM((16, rubrics, points), f32),
            pltpu.VMEM((10, rubrics, points), f32),
            pltpu.VMEM((16, rubrics, points), f32),
            pltpu.VMEM((2, 8, 128), f32),
            pltpu.VMEM((30, 8, 128), f32),
            pltpu.VMEM((2, 8, 128), f32),
            pltpu.VMEM((30, 8, 128), f32),
            dma((4,)), dma((10,)), dma((10,)), dma((9,)), dma((9,)), dma((8,)), dma((8,)),
            dma((10,)), dma((10,)), dma((16,)), dma((16,)), dma((30,)), dma((30,)), dma((30,)), dma((30,)),
        ],
        compiler_params=pltpu.CompilerParams(
            collective_id=0, has_side_effects=True, vmem_limit_bytes=56 * 2**20
        ),
        cost_estimate=pl.CostEstimate(
            flops=20_000_000_000, bytes_accessed=1_000_000, transcendentals=9_000_000
        ),
        name="iteration",
    )(embeddings, solution, residual, direction)
    return stacked[0:16], stacked[16:32], stacked[32:48]


def solution(mesh):
    spec = P(None, ("row", "col"))
    return jax.shard_map(
        shards, mesh=mesh, in_specs=(spec,) * 4, out_specs=(spec,) * 3, check_vma=False
    )
```

```python
import jax
import jax.numpy as jnp
from jax import lax
from jax.experimental import pallas as pl
from jax.experimental.pallas import tpu as pltpu
from jax.sharding import PartitionSpec as P

f32, bf16, f8 = jnp.float32, jnp.bfloat16, jnp.float8_e4m3fn
MESH = pl.DeviceIdType.MESH
highest = lax.Precision.HIGHEST

ridge_weight = 0.5
points = 256
rubrics = 16
width = 384
deep = 512
aug_at, hi_at, lo_at, rows_sent = 384, 400, 416, 432
low_scale, dir_scale, dir_step = 65536.0, 64.0, 16.0
scale = 4.0 / width

slots = [
    ((1, 0), (1, 0)),
    ((0, 3), (0, 3)),
    ((3, 1), (3, 1)),
    ((3, 2), (3, 0)),
    ((1, 1), (0, 1)),
    ((2, 1), (3, 0)),
    ((2, 0), (1, 0)),
    ((0, 2), (0, 3)),
    ((2, 2), (0, 1)),
    ((0, 0), None),
]
own = 9
others = [index for index in range(10) if index != own]
place = {offset: index for index, (offset, _) in enumerate(slots)}
along_z = [0, 1, 7, 2, 6, 3, 5, 4]
halves = ((0, 208), (208, 224))


def parent(index):
    (ox, oy), (hx, hy) = slots[index]
    return place[((ox - hx) % 4, (oy - hy) % 4)]


def nt(left, right, precision=None):
    return lax.dot_general(
        left, right, (((1,), (1,)), ((), ())), precision=precision, preferred_element_type=f32
    )


def nn(left, right):
    return jnp.dot(left, right, precision=highest, preferred_element_type=f32)


def low_parts(pieces):
    whole = pieces.astype(f32)
    whole = (whole[:rubrics] + whole[rubrics:]) * dir_scale
    first = whole.astype(f8)
    second = ((whole - first.astype(f32)) * dir_step).astype(f8)
    return jnp.concatenate([first, second], axis=0)


def combine(parts):
    low = parts[32:48] + parts[48:64] * (1.0 / dir_step)
    return parts[0:16] + parts[16:32] + low * (1.0 / (low_scale * dir_scale))


def pack(matrix):
    return jnp.concatenate([matrix[0:8], matrix[8:16]], axis=1)


def unpack(packed, at):
    return jnp.concatenate([packed[:, at : at + 16], packed[:, at + 16 : at + 32]], axis=0)


def inverse(matrix):
    row = lax.broadcasted_iota(jnp.int32, matrix.shape, 0)
    col = lax.broadcasted_iota(jnp.int32, matrix.shape, 1)
    for s in range(0, matrix.shape[0], 2):
        e = s + 1
        one, two = matrix[s:e, :], matrix[e : e + 1, :]
        col_one, col_two = matrix[:, s:e], matrix[:, e : e + 1]
        a, b, c, d = one[:, s:e], one[:, e : e + 1], two[:, s:e], two[:, e : e + 1]
        share = 1.0 / (a * d - b * c)
        first, second = col == s, col == e
        one = jnp.where(first[0:1], 1.0, jnp.where(second[0:1], 0.0, one))
        two = jnp.where(first[0:1], 0.0, jnp.where(second[0:1], 1.0, two))
        new_one = (d * share) * one - (b * share) * two
        new_two = (a * share) * two - (c * share) * one
        inner = jnp.where(first | second, 0.0, matrix) - col_one * new_one - col_two * new_two
        matrix = jnp.where(row == s, new_one, jnp.where(row == e, new_two, inner))
    return matrix


def kernel(
    e_hbm, sol_hbm, res_hbm, dir_hbm, out,
    e_ref, sol_ref, res_ref, dir_ref,
    xb, xa, la, acc_a, acc_b, part_a, part_b, sum_a, sum_b, gram, gram_in, old, old_in, curv, curv_in,
    in_sem, a_send, a_recv, z_send, z_recv, c_send, c_recv, pa_send, pa_recv, pb_send, pb_recv,
    g_send, g_recv, o_send, o_recv, q_send, q_recv,
):
    row, col = lax.axis_index("row"), lax.axis_index("col")
    core, x, z_lo = lax.rem(row, 2), lax.rem(lax.div(row, 2), 4), lax.div(row, 8)
    y, z_hi = lax.div(col, 4), lax.rem(col, 4)
    z = z_hi * 2 + z_lo

    def device(dx=0, dy=0, dz=0, dc=0):
        x2, y2 = lax.rem(x + dx % 4, 4), lax.rem(y + dy % 4, 4)
        z2, c2 = lax.rem(z + dz % 8, 8), lax.rem(core + dc, 2)
        return (lax.rem(z2, 2) * 8 + x2 * 2 + c2, y2 * 4 + lax.div(z2, 2))

    barrier = pltpu.get_barrier_semaphore()
    neighbours = [
        device(dx=1), device(dx=3), device(dy=1), device(dy=3), device(dz=1), device(dz=7), device(dc=1),
        device(dx=3, dy=1),
    ]
    for neighbour in neighbours:
        pl.semaphore_signal(barrier, inc=1, device_id=neighbour, device_id_type=MESH)
    fetch = [
        pltpu.make_async_copy(source, into, in_sem.at[n])
        for n, (source, into) in enumerate(
            ((e_hbm, e_ref), (dir_hbm, dir_ref), (res_hbm, res_ref), (sol_hbm, sol_ref))
        )
    ]
    for copy in fetch:
        copy.start()

    fetch[0].wait()
    fetch[1].wait()
    block = e_ref[...]
    wide = block.astype(f32)
    half = -0.5 * jnp.sum(wide * wide, axis=0, keepdims=True)
    h1 = half.astype(bf16).astype(f32)
    h2 = (half - h1).astype(bf16).astype(f32)
    h3 = half - h1 - h2
    at = lax.broadcasted_iota(jnp.int32, (16, points), 0)
    ones = jnp.where((at >= 8) & (at < 11), 1.0, 0.0)
    aug = jnp.where(at == 0, h1, jnp.where(at == 1, h2, jnp.where(at == 2, h3, ones)))
    way = dir_ref[...]
    way_hi = way.astype(bf16)
    way_lo = (way - way_hi.astype(f32)).astype(bf16)
    for buffer, slot in ((xb, 0), (xa, own)):
        buffer[slot, 0:width, :] = block
        buffer[slot, aug_at:hi_at, :] = aug.astype(bf16)
        buffer[slot, hi_at:lo_at, :] = way_hi
        buffer[slot, lo_at:rows_sent, :] = way_lo

    pl.semaphore_wait(barrier, len(neighbours))

    body_rows = pl.ds(0, rows_sent)

    def remote(source, target, send, recv, to):
        return pltpu.make_async_remote_copy(
            src_ref=source, dst_ref=target, send_sem=send, recv_sem=recv,
            device_id=to, device_id_type=MESH,
        )

    def a_copy(index, part):
        hx, hy = slots[index][1]
        rows = pl.ds(*halves[part])
        return remote(
            xa.at[parent(index), rows, :], xa.at[index, rows, :],
            a_send.at[index, part], a_recv.at[index, part], device(dx=-hx, dy=-hy),
        )

    def z_copy(index, part):
        source = [None, 0, 0, 1, 2, 3, 4, 5, 6][index]
        rows = pl.ds(*halves[part])
        step = -1 if index in (1, 3, 5, 7) else 1
        return remote(
            xb.at[2 * source, rows, :], xb.at[2 * min(index, 7), rows, :],
            z_send.at[index, part], z_recv.at[index, part], device(dz=step),
        )

    def z_part(index, n):
        return n if index % 2 else 1 - n

    def c_copy(slot):
        return remote(
            xb.at[2 * slot, body_rows, :], xb.at[2 * slot + 1, body_rows, :], c_send.at[slot], c_recv.at[slot],
            device(dc=1),
        )

    def turn(index):
        rows = pl.ds(index * points, points)
        la[rows, 0:width] = xa[index, 0:width, :].T
        extra = xa[index, aug_at:hi_at, :].astype(f32)
        extra = jnp.concatenate([extra[8:16], extra[0:8], jnp.zeros((112, points), f32)], axis=0)
        la[rows, width:deep] = extra.T.astype(bf16)

    for n in (0, 1):
        for index in (1, 2):
            z_copy(index, z_part(index, n)).start()
        for index in (0, 1, 2):
            a_copy(index, n).start()
    c_copy(0).start()

    turn(own)
    xb[:, rows_sent:deep, :] = jnp.zeros((16, deep - rows_sent, points), bf16)
    acc_a[...] = jnp.zeros_like(acc_a)
    acc_b[...] = jnp.zeros_like(acc_b)
    fetch[2].wait()
    fetch[3].wait()
    rest = res_ref[...]
    empty = jnp.zeros((8, 96), f32)
    old[0] = jnp.concatenate([pack(nt(rest, rest, highest)), empty], axis=1)

    def split(lhs, z_blocks):
        parts = [jnp.dot(lhs, xb[block], preferred_element_type=f32) for block in z_blocks]
        values = jnp.exp(jnp.concatenate(parts, axis=1) * scale)
        high = values.astype(bf16)
        return high, ((values - high.astype(f32)) * low_scale).astype(f8)

    def apply_rows(rows, right, right_low, high, low):
        acc_a[rows, 0:32] += nt(high, right)
        acc_a[rows, 32:64] += nt(low, right_low)

    def directions(z_blocks):
        right = jnp.concatenate([xb[block, hi_at:rows_sent, :] for block in z_blocks], axis=1)
        return right, low_parts(right)

    def both(*z_slots):
        return [block for k in z_slots for block in (2 * k, 2 * k + 1)]

    def tile(first_slots, z_blocks):
        runs = [(first * points, count * points) for first, count in first_slots]
        lhs = [la[pl.ds(*run), :] for run in runs]
        high, low = split(jnp.concatenate(lhs, axis=0) if len(lhs) > 1 else lhs[0], z_blocks)
        right, right_low = directions(z_blocks)
        start = 0
        for run in runs:
            part = slice(start, start + run[1])
            apply_rows(pl.ds(*run), right, right_low, high[part], low[part])
            start += run[1]
        left = [xa[first + n, hi_at:rows_sent, :] for first, count in first_slots for n in range(count)]
        left = jnp.concatenate(left, axis=1) if len(left) > 1 else left[0]
        by_high = jnp.dot(left, high, preferred_element_type=f32)
        by_low = jnp.dot(low_parts(left), low, preferred_element_type=f32)
        for n, block in enumerate(z_blocks):
            lanes = slice(n * points, (n + 1) * points)
            acc_b[block, 0:32, :] += by_high[:, lanes]
            acc_b[block, 32:64, :] += by_low[:, lanes]

    def own_tile(z_blocks):
        rows = pl.ds(own * points, points)
        apply_rows(rows, *directions(z_blocks), *split(la[rows, :], z_blocks))

    low_x, low_y = x < 2, y < 2
    mine = jnp.where(low_x, 0, 1)
    mine_other = jnp.where(low_x == low_y, 0, 1)

    def b_copy(slot):
        return remote(
            part_b.at[slot], sum_b.at[slot], pb_send.at[slot], pb_recv.at[slot],
            device(dz=along_z[slot // 2], dc=slot % 2),
        )

    def hand_b(*which):
        for k in which:
            for slot in (2 * k, 2 * k + 1):
                part_b[slot] = combine(acc_b[slot])
                if slot:
                    b_copy(slot).start()

    def pa_copy(index):
        ox, oy = slots[index][0]
        return remote(
            part_a.at[index], sum_a.at[index], pa_send.at[index], pa_recv.at[index], device(dx=ox, dy=oy)
        )

    def hand_a(*which):
        for index in which:
            part_a[index] = combine(acc_a[pl.ds(index * points, points), :].T)
            if index != own:
                pa_copy(index).start()

    def sum_copies(sent, landed, send, recv):
        plane = sorted(range(1, 16), key=lambda o: -min(o // 4, 4 - o // 4) - min(o % 4, 4 - o % 4))
        column = sorted(range(1, 16), key=lambda o: -min(o // 2, 8 - o // 2))
        targets = [device(dx=o // 4, dy=o % 4) for o in plane]
        targets += [device(dz=o // 2, dc=o % 2) for o in column]
        return [
            remote(sent.at[n // 15], landed.at[n], send.at[n], recv.at[n], to) for n, to in enumerate(targets)
        ]

    def start_stage(copies, stage):
        for copy in copies[15 * stage : 15 * stage + 15]:
            copy.start()

    def finish_stage(copies, sent, landed, stage):
        total = sent[stage]
        for n in range(15 * stage, 15 * stage + 15):
            copies[n].wait_recv()
            total = total + landed[n]
        return total

    old_copies = sum_copies(old, old_in, o_send, o_recv)
    gram_copies = sum_copies(gram, gram_in, g_send, g_recv)
    curv_copies = sum_copies(curv, curv_in, q_send, q_recv)

    def relay(n, z_in, z_out, a_in, a_out):
        for index in z_in:
            z_copy(index, z_part(index, n)).wait_recv()
        for index in z_out:
            z_copy(index, z_part(index, n)).start()
        if n == 1:
            for slot in z_in:
                c_copy(slot).start()
        for index in a_in:
            a_copy(index, n).wait_recv()
        for index in a_out:
            a_copy(index, n).start()

    def siblings(*which):
        for slot in which:
            c_copy(slot).wait_recv()

    def old_first():
        start_stage(old_copies, 0)

    def old_second():
        old[1] = finish_stage(old_copies, old, old_in, 0)
        start_stage(old_copies, 1)

    for n in (0, 1):
        relay(n, (1, 2), (3, 4), (0, 1, 2), (7, 4, 5, 6))
    for index in (0, 1, 2):
        turn(index)
    siblings(0)
    tile([(0, 3)], both(0))
    siblings(1, 2)
    own_tile(both(0, 1))
    relay(0, (3, 4), (5, 6), (7, 4, 5, 6), (3, 8))
    tile([(0, 3)], both(1, 2))
    relay(1, (3, 4), (5, 6), (7, 4, 5, 6), (3, 8))
    for index in (4, 5, 6, 7):
        turn(index)
    tile([(4, 2)], both(0, 1, 2))
    old_first()
    siblings(3, 4)
    relay(0, (5, 6), (7, 8), (3, 8), ())
    tile([(0, 2), (4, 2)], both(3, 4))
    own_tile(both(2))
    relay(1, (5, 6), (), (3, 8), ())
    for index in (3, 8):
        turn(index)
    tile([(3, 1)], both(0, 1, 2))
    hand_b(2)
    tile([(2, 2)], both(3, 4))
    hand_b(4)
    siblings(5, 6)
    tile([(0, 2), (4, 2)], both(5, 6))
    for index in (7, 8):
        z_copy(index, z_part(index, 0)).wait_recv()
    c_copy(7).start()
    old_second()
    tile([(8, 1)], both(1, 3))
    siblings(7)
    tile([(0, 6)], both(7))
    hand_a(4, 5, 0, 1)
    tile([(8, 1)], both(5) + [mine, 14 + mine])
    hand_a(8)
    tile([(6, 2)], both(5) + [mine_other, 14 + mine_other])
    hand_b(7, 0)
    tile([(2, 2)], both(5, 6))
    hand_a(3, 2)
    hand_b(5, 6)
    tile([(6, 2)], both(1, 3))
    hand_a(6, 7)
    hand_b(3, 1)
    own_tile(both(3, 4))
    own_tile(both(5, 6, 7))
    hand_a(own)

    ways = [
        xa[index, hi_at:lo_at, :].astype(f32) + xa[index, lo_at:rows_sent, :].astype(f32) for index in others
    ]
    partials = [part_a[index] for index in others]
    held = nt(jnp.concatenate(ways, axis=1), jnp.concatenate(partials, axis=1), highest)
    held = held + 0.5 * nt(way, part_a[own] + ridge_weight * way, highest)
    curv[0] = jnp.concatenate([pack(held + held.T), empty], axis=1)
    start_stage(curv_copies, 0)

    rr = unpack(finish_stage(old_copies, old, old_in, 1), 0)
    rr_inv = inverse(rr)
    product = part_a[own] + part_b[0] + ridge_weight * way
    for slot in (4, 5, 8, 9, 14, 15, 1, 10, 11, 12, 13):
        b_copy(slot).wait_recv()
        product = product + sum_b[slot]
    for index in (0, 1, 4, 5, 8, 2, 3, 6, 7):
        pa_copy(index).wait_recv()
        product = product + sum_a[index]
    for slot in (2, 3, 6, 7):
        b_copy(slot).wait_recv()
        product = product + sum_b[slot]

    with_rest = nt(product, jnp.concatenate([product, rest], axis=0), highest)
    gram[0] = jnp.concatenate([pack(with_rest[:, 16:32]), pack(with_rest[:, 0:16]), empty[:, 0:64]], axis=1)
    start_stage(gram_copies, 0)
    curv[1] = finish_stage(curv_copies, curv, curv_in, 0)
    start_stage(curv_copies, 1)
    gram[1] = finish_stage(gram_copies, gram, gram_in, 0)
    start_stage(gram_copies, 1)

    curvature_inv = inverse(unpack(finish_stage(curv_copies, curv, curv_in, 1), 0))
    alpha_t = nn(rr, curvature_inv)
    turned = nn(jnp.concatenate([curvature_inv, rr_inv], axis=0), way)
    residual_next = rest - nn(alpha_t, product)
    out[16:32] = residual_next
    out[0:16] = sol_ref[...] + nn(alpha_t, way)
    moved = residual_next + way

    total = finish_stage(gram_copies, gram, gram_in, 1)
    pr, pp = unpack(total, 0), unpack(total, 32)
    inner = nn(jnp.concatenate([pp, -pr], axis=1), turned)
    out[32:48] = moved + nn(alpha_t, inner) - nn(pr.T, turned[0:16])

    for index in others:
        pa_copy(index).wait_send()
        for part in (0, 1):
            a_copy(index, part).wait_send()
    for index in range(1, 9):
        for n in (0, 1) if index < 7 else (0,):
            z_copy(index, z_part(index, n)).wait_send()
    for slot in range(8):
        c_copy(slot).wait_send()
    for slot in range(1, 16):
        b_copy(slot).wait_send()
    for copy in old_copies + gram_copies + curv_copies:
        copy.wait_send()


def shards(embeddings, solution, residual, direction):
    vmem = pl.BlockSpec(memory_space=pltpu.VMEM)
    dma = pltpu.SemaphoreType.DMA
    stacked = pl.pallas_call(
        kernel,
        out_shape=jax.ShapeDtypeStruct((3 * rubrics, points), f32),
        in_specs=[pl.BlockSpec(memory_space=pl.ANY)] * 4,
        out_specs=vmem,
        scratch_shapes=[
            pltpu.VMEM((width, points), bf16),
            pltpu.VMEM((rubrics, points), f32),
            pltpu.VMEM((rubrics, points), f32),
            pltpu.VMEM((rubrics, points), f32),
            pltpu.VMEM((16, deep, points), bf16),
            pltpu.VMEM((10, rows_sent, points), bf16),
            pltpu.VMEM((10 * points, deep), bf16),
            pltpu.VMEM((10 * points, 64), f32),
            pltpu.VMEM((16, 64, points), f32),
            pltpu.VMEM((10, rubrics, points), f32),
            pltpu.VMEM((16, rubrics, points), f32),
            pltpu.VMEM((10, rubrics, points), f32),
            pltpu.VMEM((16, rubrics, points), f32),
            pltpu.VMEM((2, 8, 128), f32),
            pltpu.VMEM((30, 8, 128), f32),
            pltpu.VMEM((2, 8, 128), f32),
            pltpu.VMEM((30, 8, 128), f32),
            pltpu.VMEM((2, 8, 128), f32),
            pltpu.VMEM((30, 8, 128), f32),
            dma((4,)), dma((10, 2)), dma((10, 2)), dma((9, 2)), dma((9, 2)), dma((8,)), dma((8,)),
            dma((10,)), dma((10,)), dma((16,)), dma((16,)), dma((30,)), dma((30,)), dma((30,)), dma((30,)),
            dma((30,)), dma((30,)),
        ],
        compiler_params=pltpu.CompilerParams(
            collective_id=0, has_side_effects=True, vmem_limit_bytes=56 * 2**20
        ),
        cost_estimate=pl.CostEstimate(
            flops=20_000_000_000, bytes_accessed=1_000_000, transcendentals=9_000_000
        ),
        name="iteration",
    )(embeddings, solution, residual, direction)
    return stacked[0:16], stacked[16:32], stacked[32:48]


def solution(mesh):
    spec = P(None, ("row", "col"))
    return jax.shard_map(
        shards, mesh=mesh, in_specs=(spec,) * 4, out_specs=(spec,) * 3, check_vma=False
    )
```

```python
import jax
import jax.numpy as jnp
from jax import lax
from jax.experimental import pallas as pl
from jax.experimental.pallas import tpu as pltpu
from jax.sharding import PartitionSpec as P

f32, bf16, f8 = jnp.float32, jnp.bfloat16, jnp.float8_e4m3fn
MESH = pl.DeviceIdType.MESH
highest = lax.Precision.HIGHEST

ridge_weight = 0.5
points = 256
rubrics = 16
width = 384
deep = 512
aug_at, hi_at, lo_at, rows_sent = 384, 400, 416, 432
low_scale, dir_scale, dir_step = 65536.0, 64.0, 16.0
scale = 4.0 / width

slots = [
    ((1, 0), (1, 0)),
    ((0, 3), (0, 3)),
    ((3, 1), (3, 1)),
    ((3, 2), (3, 0)),
    ((1, 1), (0, 1)),
    ((2, 1), (3, 0)),
    ((2, 0), (1, 0)),
    ((0, 2), (0, 3)),
    ((2, 2), (0, 1)),
    ((0, 0), None),
]
own = 9
others = [index for index in range(10) if index != own]
place = {offset: index for index, (offset, _) in enumerate(slots)}
along_z = [0, 1, 7, 2, 6, 3, 5, 4]
halves = ((0, 208), (208, 224))


def parent(index):
    (ox, oy), (hx, hy) = slots[index]
    return place[((ox - hx) % 4, (oy - hy) % 4)]


def nt(left, right, precision=None):
    return lax.dot_general(
        left, right, (((1,), (1,)), ((), ())), precision=precision, preferred_element_type=f32
    )


def nn(left, right):
    return jnp.dot(left, right, precision=highest, preferred_element_type=f32)


def low_parts(pieces):
    whole = pieces.astype(f32)
    whole = (whole[:rubrics] + whole[rubrics:]) * dir_scale
    first = whole.astype(f8)
    second = ((whole - first.astype(f32)) * dir_step).astype(f8)
    return jnp.concatenate([first, second], axis=0)


def combine(parts):
    low = parts[32:48] + parts[48:64] * (1.0 / dir_step)
    return parts[0:16] + parts[16:32] + low * (1.0 / (low_scale * dir_scale))


def pack(matrix):
    return jnp.concatenate([matrix[0:8], matrix[8:16]], axis=1)


def unpack(packed, at):
    return jnp.concatenate([packed[:, at : at + 16], packed[:, at + 16 : at + 32]], axis=0)


def inverse(matrix):
    row = lax.broadcasted_iota(jnp.int32, matrix.shape, 0)
    col = lax.broadcasted_iota(jnp.int32, matrix.shape, 1)
    for s in range(0, matrix.shape[0], 2):
        e = s + 1
        one, two = matrix[s:e, :], matrix[e : e + 1, :]
        col_one, col_two = matrix[:, s:e], matrix[:, e : e + 1]
        a, b, c, d = one[:, s:e], one[:, e : e + 1], two[:, s:e], two[:, e : e + 1]
        share = 1.0 / (a * d - b * c)
        first, second = col == s, col == e
        one = jnp.where(first[0:1], 1.0, jnp.where(second[0:1], 0.0, one))
        two = jnp.where(first[0:1], 0.0, jnp.where(second[0:1], 1.0, two))
        new_one = (d * share) * one - (b * share) * two
        new_two = (a * share) * two - (c * share) * one
        inner = jnp.where(first | second, 0.0, matrix) - col_one * new_one - col_two * new_two
        matrix = jnp.where(row == s, new_one, jnp.where(row == e, new_two, inner))
    return matrix


def kernel(
    e_hbm, sol_hbm, res_hbm, dir_hbm, out,
    e_ref, sol_ref, res_ref, dir_ref,
    xb, xa, la, acc_a, acc_b, part_a, part_b, sum_a, sum_b, gram, gram_in, old, old_in, curv, curv_in,
    in_sem, a_send, a_recv, z_send, z_recv, c_send, c_recv, pa_send, pa_recv, pb_send, pb_recv,
    g_send, g_recv, o_send, o_recv, q_send, q_recv,
):
    row, col = lax.axis_index("row"), lax.axis_index("col")
    core, x, z_lo = lax.rem(row, 2), lax.rem(lax.div(row, 2), 4), lax.div(row, 8)
    y, z_hi = lax.div(col, 4), lax.rem(col, 4)
    z = z_hi * 2 + z_lo

    def device(dx=0, dy=0, dz=0, dc=0):
        x2, y2 = lax.rem(x + dx % 4, 4), lax.rem(y + dy % 4, 4)
        z2, c2 = lax.rem(z + dz % 8, 8), lax.rem(core + dc, 2)
        return (lax.rem(z2, 2) * 8 + x2 * 2 + c2, y2 * 4 + lax.div(z2, 2))

    barrier = pltpu.get_barrier_semaphore()
    neighbours = [
        device(dx=1), device(dx=3), device(dy=1), device(dy=3), device(dz=1), device(dz=7), device(dc=1),
        device(dx=3, dy=1),
    ]
    for neighbour in neighbours:
        pl.semaphore_signal(barrier, inc=1, device_id=neighbour, device_id_type=MESH)
    fetch = [
        pltpu.make_async_copy(source, into, in_sem.at[n])
        for n, (source, into) in enumerate(
            ((e_hbm, e_ref), (dir_hbm, dir_ref), (res_hbm, res_ref), (sol_hbm, sol_ref))
        )
    ]
    for copy in fetch:
        copy.start()

    fetch[0].wait()
    fetch[1].wait()
    block = e_ref[...]
    wide = block.astype(f32)
    half = -0.5 * jnp.sum(wide * wide, axis=0, keepdims=True)
    h1 = half.astype(bf16).astype(f32)
    h2 = (half - h1).astype(bf16).astype(f32)
    h3 = half - h1 - h2
    at = lax.broadcasted_iota(jnp.int32, (16, points), 0)
    ones = jnp.where((at >= 8) & (at < 11), 1.0, 0.0)
    aug = jnp.where(at == 0, h1, jnp.where(at == 1, h2, jnp.where(at == 2, h3, ones)))
    way = dir_ref[...]
    way_hi = way.astype(bf16)
    way_lo = (way - way_hi.astype(f32)).astype(bf16)
    for buffer, slot in ((xb, 0), (xa, own)):
        buffer[slot, 0:width, :] = block
        buffer[slot, aug_at:hi_at, :] = aug.astype(bf16)
        buffer[slot, hi_at:lo_at, :] = way_hi
        buffer[slot, lo_at:rows_sent, :] = way_lo

    pl.semaphore_wait(barrier, len(neighbours))

    body_rows = pl.ds(0, rows_sent)

    def remote(source, target, send, recv, to):
        return pltpu.make_async_remote_copy(
            src_ref=source, dst_ref=target, send_sem=send, recv_sem=recv,
            device_id=to, device_id_type=MESH,
        )

    def a_copy(index, part):
        hx, hy = slots[index][1]
        rows = pl.ds(*halves[part])
        return remote(
            xa.at[parent(index), rows, :], xa.at[index, rows, :],
            a_send.at[index, part], a_recv.at[index, part], device(dx=-hx, dy=-hy),
        )

    def z_copy(index, part):
        source = [None, 0, 0, 1, 2, 3, 4, 5, 6][index]
        rows = pl.ds(*halves[part])
        step = -1 if index in (1, 3, 5, 7) else 1
        return remote(
            xb.at[2 * source, rows, :], xb.at[2 * min(index, 7), rows, :],
            z_send.at[index, part], z_recv.at[index, part], device(dz=step),
        )

    def z_part(index, n):
        return n if index % 2 else 1 - n

    def c_copy(slot):
        return remote(
            xb.at[2 * slot, body_rows, :], xb.at[2 * slot + 1, body_rows, :], c_send.at[slot], c_recv.at[slot],
            device(dc=1),
        )

    def turn(index):
        rows = pl.ds(index * points, points)
        la[rows, 0:width] = xa[index, 0:width, :].T
        extra = xa[index, aug_at:hi_at, :].astype(f32)
        extra = jnp.concatenate([extra[8:16], extra[0:8], jnp.zeros((112, points), f32)], axis=0)
        la[rows, width:deep] = extra.T.astype(bf16)

    for n in (0, 1):
        for index in (1, 2):
            z_copy(index, z_part(index, n)).start()
        for index in (0, 1, 2):
            a_copy(index, n).start()
    c_copy(0).start()

    turn(own)
    xb[:, rows_sent:deep, :] = jnp.zeros((16, deep - rows_sent, points), bf16)
    acc_a[...] = jnp.zeros_like(acc_a)
    acc_b[...] = jnp.zeros_like(acc_b)
    fetch[2].wait()
    fetch[3].wait()
    rest = res_ref[...]
    empty = jnp.zeros((8, 96), f32)
    old[0] = jnp.concatenate([pack(nt(rest, rest, highest)), empty], axis=1)

    def split(lhs, z_blocks):
        parts = [jnp.dot(lhs, xb[block], preferred_element_type=f32) for block in z_blocks]
        values = jnp.exp(jnp.concatenate(parts, axis=1) * scale)
        high = values.astype(bf16)
        return high, ((values - high.astype(f32)) * low_scale).astype(f8)

    def apply_rows(rows, right, right_low, high, low):
        acc_a[rows, 0:32] += nt(high, right)
        acc_a[rows, 32:64] += nt(low, right_low)

    def directions(z_blocks):
        right = jnp.concatenate([xb[block, hi_at:rows_sent, :] for block in z_blocks], axis=1)
        return right, low_parts(right)

    def both(*z_slots):
        return [block for k in z_slots for block in (2 * k, 2 * k + 1)]

    def tile(first_slots, z_blocks):
        runs = [(first * points, count * points) for first, count in first_slots]
        lhs = [la[pl.ds(*run), :] for run in runs]
        high, low = split(jnp.concatenate(lhs, axis=0) if len(lhs) > 1 else lhs[0], z_blocks)
        right, right_low = directions(z_blocks)
        start = 0
        for run in runs:
            part = slice(start, start + run[1])
            apply_rows(pl.ds(*run), right, right_low, high[part], low[part])
            start += run[1]
        left = [xa[first + n, hi_at:rows_sent, :] for first, count in first_slots for n in range(count)]
        left = jnp.concatenate(left, axis=1) if len(left) > 1 else left[0]
        by_high = jnp.dot(left, high, preferred_element_type=f32)
        by_low = jnp.dot(low_parts(left), low, preferred_element_type=f32)
        for n, block in enumerate(z_blocks):
            lanes = slice(n * points, (n + 1) * points)
            acc_b[block, 0:32, :] += by_high[:, lanes]
            acc_b[block, 32:64, :] += by_low[:, lanes]

    def own_tile(z_blocks):
        rows = pl.ds(own * points, points)
        apply_rows(rows, *directions(z_blocks), *split(la[rows, :], z_blocks))

    low_x, low_y = x < 2, y < 2
    mine = jnp.where(low_x, 0, 1)
    mine_other = jnp.where(low_x == low_y, 0, 1)

    def b_copy(slot):
        return remote(
            part_b.at[slot], sum_b.at[slot], pb_send.at[slot], pb_recv.at[slot],
            device(dz=along_z[slot // 2], dc=slot % 2),
        )

    def hand_b(*which):
        for k in which:
            for slot in (2 * k, 2 * k + 1):
                part_b[slot] = combine(acc_b[slot])
                if slot:
                    b_copy(slot).start()

    def pa_copy(index):
        ox, oy = slots[index][0]
        return remote(
            part_a.at[index], sum_a.at[index], pa_send.at[index], pa_recv.at[index], device(dx=ox, dy=oy)
        )

    def hand_a(*which):
        for index in which:
            part_a[index] = combine(acc_a[pl.ds(index * points, points), :].T)
            if index != own:
                pa_copy(index).start()

    def sum_copies(sent, landed, send, recv):
        plane = sorted(range(1, 16), key=lambda o: -min(o // 4, 4 - o // 4) - min(o % 4, 4 - o % 4))
        column = sorted(range(1, 16), key=lambda o: -min(o // 2, 8 - o // 2))
        targets = [device(dx=o // 4, dy=o % 4) for o in plane]
        targets += [device(dz=o // 2, dc=o % 2) for o in column]
        return [
            remote(sent.at[n // 15], landed.at[n], send.at[n], recv.at[n], to) for n, to in enumerate(targets)
        ]

    def start_stage(copies, stage):
        for copy in copies[15 * stage : 15 * stage + 15]:
            copy.start()

    def finish_stage(copies, sent, landed, stage):
        total = sent[stage]
        for n in range(15 * stage, 15 * stage + 15):
            copies[n].wait_recv()
            total = total + landed[n]
        return total

    old_copies = sum_copies(old, old_in, o_send, o_recv)
    gram_copies = sum_copies(gram, gram_in, g_send, g_recv)
    curv_copies = sum_copies(curv, curv_in, q_send, q_recv)

    def relay(n, z_in, z_out, a_in, a_out):
        for index in z_in:
            z_copy(index, z_part(index, n)).wait_recv()
        for index in z_out:
            z_copy(index, z_part(index, n)).start()
        if n == 1:
            for slot in z_in:
                c_copy(slot).start()
        for index in a_in:
            a_copy(index, n).wait_recv()
            for onward in a_out:
                if parent(onward) == index:
                    a_copy(onward, n).start()

    def siblings(*which):
        for slot in which:
            c_copy(slot).wait_recv()

    def old_first():
        start_stage(old_copies, 0)

    def old_second():
        old[1] = finish_stage(old_copies, old, old_in, 0)
        start_stage(old_copies, 1)

    for n in (0, 1):
        relay(n, (1, 2), (3, 4), (0, 1, 2), (7, 4, 5, 6))
    for index in (0, 1, 2):
        turn(index)
    siblings(0)
    tile([(0, 3)], both(0))
    relay(0, (3, 4), (5, 6), (7, 4, 5, 6), (3, 8))
    siblings(1, 2)
    own_tile(both(0, 1))
    tile([(0, 3)], both(1, 2))
    relay(1, (3, 4), (5, 6), (7, 4, 5, 6), (3, 8))
    for index in (4, 5):
        turn(index)
    tile([(4, 2)], both(0, 1, 2))
    relay(0, (5, 6), (7, 8), (3, 8), ())
    old_first()
    siblings(3, 4)
    tile([(0, 2), (4, 2)], both(3, 4))
    relay(1, (5, 6), (), (3, 8), ())
    turn(3)
    tile([(3, 1)], both(0, 1, 2))
    hand_b(2)
    tile([(2, 2)], both(3, 4))
    hand_b(4)
    for index in (7, 8):
        z_copy(index, z_part(index, 0)).wait_recv()
    c_copy(7).start()
    siblings(5, 6)
    tile([(0, 2), (4, 2)], both(5, 6))
    old_second()
    turn(8)
    tile([(8, 1)], both(1, 3))
    siblings(7)
    tile([(0, 6)], both(7))
    turn(6)
    turn(7)
    hand_a(4, 5, 0, 1)
    tile([(8, 1)], both(5) + [mine, 14 + mine])
    hand_a(8)
    tile([(6, 2)], both(5) + [mine_other, 14 + mine_other])
    hand_b(7, 0)
    tile([(2, 2)], both(5, 6))
    hand_a(3, 2)
    hand_b(5, 6)
    tile([(6, 2)], both(1, 3))
    hand_a(6, 7)
    hand_b(3, 1)
    own_tile(both(2, 3, 4))
    own_tile(both(5, 6, 7))
    hand_a(own)

    ways = [
        xa[index, hi_at:lo_at, :].astype(f32) + xa[index, lo_at:rows_sent, :].astype(f32) for index in others
    ]
    partials = [part_a[index] for index in others]
    held = nt(jnp.concatenate(ways, axis=1), jnp.concatenate(partials, axis=1), highest)
    held = held + 0.5 * nt(way, part_a[own] + ridge_weight * way, highest)
    curv[0] = jnp.concatenate([pack(held + held.T), empty], axis=1)
    start_stage(curv_copies, 0)

    product = part_a[own] + part_b[0] + ridge_weight * way
    for slot in (4, 5, 8, 9, 14, 15, 1, 10, 11, 12, 13):
        b_copy(slot).wait_recv()
        product = product + sum_b[slot]
    for index in (0, 1, 4, 5, 8, 2, 3, 6, 7):
        pa_copy(index).wait_recv()
        product = product + sum_a[index]
    for slot in (2, 3, 6, 7):
        b_copy(slot).wait_recv()
        product = product + sum_b[slot]

    with_rest = nt(product, jnp.concatenate([product, rest], axis=0), highest)
    gram[0] = jnp.concatenate([pack(with_rest[:, 16:32]), pack(with_rest[:, 0:16]), empty[:, 0:64]], axis=1)
    start_stage(gram_copies, 0)
    curv[1] = finish_stage(curv_copies, curv, curv_in, 0)
    start_stage(curv_copies, 1)
    rr = unpack(finish_stage(old_copies, old, old_in, 1), 0)
    rr_inv = inverse(rr)
    gram[1] = finish_stage(gram_copies, gram, gram_in, 0)
    start_stage(gram_copies, 1)

    curvature_inv = inverse(unpack(finish_stage(curv_copies, curv, curv_in, 1), 0))
    alpha_t = nn(rr, curvature_inv)
    turned = nn(jnp.concatenate([curvature_inv, rr_inv], axis=0), way)
    residual_next = rest - nn(alpha_t, product)
    out[16:32] = residual_next
    out[0:16] = sol_ref[...] + nn(alpha_t, way)
    moved = residual_next + way

    total = finish_stage(gram_copies, gram, gram_in, 1)
    pr, pp = unpack(total, 0), unpack(total, 32)
    inner = nn(jnp.concatenate([pp, -pr], axis=1), turned)
    out[32:48] = moved + nn(alpha_t, inner) - nn(pr.T, turned[0:16])

    for index in others:
        pa_copy(index).wait_send()
        for part in (0, 1):
            a_copy(index, part).wait_send()
    for index in range(1, 9):
        for n in (0, 1) if index < 7 else (0,):
            z_copy(index, z_part(index, n)).wait_send()
    for slot in range(8):
        c_copy(slot).wait_send()
    for slot in range(1, 16):
        b_copy(slot).wait_send()
    for copy in old_copies + gram_copies + curv_copies:
        copy.wait_send()


def shards(embeddings, solution, residual, direction):
    vmem = pl.BlockSpec(memory_space=pltpu.VMEM)
    dma = pltpu.SemaphoreType.DMA
    stacked = pl.pallas_call(
        kernel,
        out_shape=jax.ShapeDtypeStruct((3 * rubrics, points), f32),
        in_specs=[pl.BlockSpec(memory_space=pl.ANY)] * 4,
        out_specs=vmem,
        scratch_shapes=[
            pltpu.VMEM((width, points), bf16),
            pltpu.VMEM((rubrics, points), f32),
            pltpu.VMEM((rubrics, points), f32),
            pltpu.VMEM((rubrics, points), f32),
            pltpu.VMEM((16, deep, points), bf16),
            pltpu.VMEM((10, rows_sent, points), bf16),
            pltpu.VMEM((10 * points, deep), bf16),
            pltpu.VMEM((10 * points, 64), f32),
            pltpu.VMEM((16, 64, points), f32),
            pltpu.VMEM((10, rubrics, points), f32),
            pltpu.VMEM((16, rubrics, points), f32),
            pltpu.VMEM((10, rubrics, points), f32),
            pltpu.VMEM((16, rubrics, points), f32),
            pltpu.VMEM((2, 8, 128), f32),
            pltpu.VMEM((30, 8, 128), f32),
            pltpu.VMEM((2, 8, 128), f32),
            pltpu.VMEM((30, 8, 128), f32),
            pltpu.VMEM((2, 8, 128), f32),
            pltpu.VMEM((30, 8, 128), f32),
            dma((4,)), dma((10, 2)), dma((10, 2)), dma((9, 2)), dma((9, 2)), dma((8,)), dma((8,)),
            dma((10,)), dma((10,)), dma((16,)), dma((16,)), dma((30,)), dma((30,)), dma((30,)), dma((30,)),
            dma((30,)), dma((30,)),
        ],
        compiler_params=pltpu.CompilerParams(
            collective_id=0, has_side_effects=True, vmem_limit_bytes=56 * 2**20
        ),
        cost_estimate=pl.CostEstimate(
            flops=20_000_000_000, bytes_accessed=1_000_000, transcendentals=9_000_000
        ),
        name="iteration",
    )(embeddings, solution, residual, direction)
    return stacked[0:16], stacked[16:32], stacked[32:48]


def solution(mesh):
    spec = P(None, ("row", "col"))
    return jax.shard_map(
        shards, mesh=mesh, in_specs=(spec,) * 4, out_specs=(spec,) * 3, check_vma=False
    )
```

```python
import jax
import jax.numpy as jnp
from jax import lax
from jax.experimental import pallas as pl
from jax.experimental.pallas import tpu as pltpu
from jax.sharding import PartitionSpec as P

f32, bf16, f8 = jnp.float32, jnp.bfloat16, jnp.float8_e4m3fn
MESH = pl.DeviceIdType.MESH
highest = lax.Precision.HIGHEST

ridge_weight = 0.5
points = 256
rubrics = 16
width = 384
deep = 512
aug_at, hi_at, lo_at, rows_sent = 384, 400, 416, 432
low_scale, dir_scale, dir_step = 65536.0, 64.0, 16.0
scale = 4.0 / width

slots = [
    ((1, 0), (1, 0)),
    ((0, 3), (0, 3)),
    ((3, 1), (3, 1)),
    ((3, 2), (3, 0)),
    ((1, 1), (0, 1)),
    ((2, 1), (3, 0)),
    ((2, 0), (1, 0)),
    ((0, 2), (0, 3)),
    ((2, 2), (0, 1)),
    ((0, 0), None),
]
own = 9
others = [index for index in range(10) if index != own]
place = {offset: index for index, (offset, _) in enumerate(slots)}
along_z = [0, 1, 7, 2, 6, 3, 5, 4]
halves = ((0, 208), (208, 224))


def parent(index):
    (ox, oy), (hx, hy) = slots[index]
    return place[((ox - hx) % 4, (oy - hy) % 4)]


def nt(left, right, precision=None):
    return lax.dot_general(
        left, right, (((1,), (1,)), ((), ())), precision=precision, preferred_element_type=f32
    )


def nn(left, right):
    return jnp.dot(left, right, precision=highest, preferred_element_type=f32)


def low_parts(pieces):
    whole = pieces.astype(f32)
    whole = (whole[:rubrics] + whole[rubrics:]) * dir_scale
    first = whole.astype(f8)
    second = ((whole - first.astype(f32)) * dir_step).astype(f8)
    return jnp.concatenate([first, second], axis=0)


def combine(parts):
    low = parts[32:48] + parts[48:64] * (1.0 / dir_step)
    return parts[0:16] + parts[16:32] + low * (1.0 / (low_scale * dir_scale))


def pack(matrix):
    return jnp.concatenate([matrix[0:8], matrix[8:16]], axis=1)


def unpack(packed, at):
    return jnp.concatenate([packed[:, at : at + 16], packed[:, at + 16 : at + 32]], axis=0)


def inverse(matrix):
    row = lax.broadcasted_iota(jnp.int32, matrix.shape, 0)
    col = lax.broadcasted_iota(jnp.int32, matrix.shape, 1)
    for s in range(0, matrix.shape[0], 2):
        e = s + 1
        one, two = matrix[s:e, :], matrix[e : e + 1, :]
        col_one, col_two = matrix[:, s:e], matrix[:, e : e + 1]
        a, b, c, d = one[:, s:e], one[:, e : e + 1], two[:, s:e], two[:, e : e + 1]
        share = 1.0 / (a * d - b * c)
        first, second = col == s, col == e
        one = jnp.where(first[0:1], 1.0, jnp.where(second[0:1], 0.0, one))
        two = jnp.where(first[0:1], 0.0, jnp.where(second[0:1], 1.0, two))
        new_one = (d * share) * one - (b * share) * two
        new_two = (a * share) * two - (c * share) * one
        inner = jnp.where(first | second, 0.0, matrix) - col_one * new_one - col_two * new_two
        matrix = jnp.where(row == s, new_one, jnp.where(row == e, new_two, inner))
    return matrix


def kernel(
    e_hbm, sol_hbm, res_hbm, dir_hbm, out,
    e_ref, sol_ref, res_ref, dir_ref,
    xb, xa, la, acc_a, acc_b, part_a, part_b, sum_a, sum_b, gram, gram_in, old, old_in, curv, curv_in,
    in_sem, a_send, a_recv, z_send, z_recv, c_send, c_recv, pa_send, pa_recv, pb_send, pb_recv,
    g_send, g_recv, o_send, o_recv, q_send, q_recv,
):
    row, col = lax.axis_index("row"), lax.axis_index("col")
    core, x, z_lo = lax.rem(row, 2), lax.rem(lax.div(row, 2), 4), lax.div(row, 8)
    y, z_hi = lax.div(col, 4), lax.rem(col, 4)
    z = z_hi * 2 + z_lo

    def device(dx=0, dy=0, dz=0, dc=0):
        x2, y2 = lax.rem(x + dx % 4, 4), lax.rem(y + dy % 4, 4)
        z2, c2 = lax.rem(z + dz % 8, 8), lax.rem(core + dc, 2)
        return (lax.rem(z2, 2) * 8 + x2 * 2 + c2, y2 * 4 + lax.div(z2, 2))

    barrier = pltpu.get_barrier_semaphore()
    neighbours = [
        device(dx=1), device(dx=3), device(dy=1), device(dy=3), device(dz=1), device(dz=7), device(dc=1),
        device(dx=3, dy=1),
    ]
    for neighbour in neighbours:
        pl.semaphore_signal(barrier, inc=1, device_id=neighbour, device_id_type=MESH)
    fetch = [
        pltpu.make_async_copy(source, into, in_sem.at[n])
        for n, (source, into) in enumerate(
            ((e_hbm, e_ref), (dir_hbm, dir_ref), (res_hbm, res_ref), (sol_hbm, sol_ref))
        )
    ]
    for copy in fetch:
        copy.start()

    fetch[0].wait()
    fetch[1].wait()
    block = e_ref[...]
    wide = block.astype(f32)
    half = -0.5 * jnp.sum(wide * wide, axis=0, keepdims=True)
    h1 = half.astype(bf16).astype(f32)
    h2 = (half - h1).astype(bf16).astype(f32)
    h3 = half - h1 - h2
    at = lax.broadcasted_iota(jnp.int32, (16, points), 0)
    ones = jnp.where((at >= 8) & (at < 11), 1.0, 0.0)
    aug = jnp.where(at == 0, h1, jnp.where(at == 1, h2, jnp.where(at == 2, h3, ones)))
    way = dir_ref[...]
    way_hi = way.astype(bf16)
    way_lo = (way - way_hi.astype(f32)).astype(bf16)
    for buffer, slot in ((xb, 0), (xa, own)):
        buffer[slot, 0:width, :] = block
        buffer[slot, aug_at:hi_at, :] = aug.astype(bf16)
        buffer[slot, hi_at:lo_at, :] = way_hi
        buffer[slot, lo_at:rows_sent, :] = way_lo

    pl.semaphore_wait(barrier, len(neighbours))

    body_rows = pl.ds(0, rows_sent)

    def remote(source, target, send, recv, to):
        return pltpu.make_async_remote_copy(
            src_ref=source, dst_ref=target, send_sem=send, recv_sem=recv,
            device_id=to, device_id_type=MESH,
        )

    def a_copy(index, part):
        hx, hy = slots[index][1]
        rows = pl.ds(*halves[part])
        return remote(
            xa.at[parent(index), rows, :], xa.at[index, rows, :],
            a_send.at[index, part], a_recv.at[index, part], device(dx=-hx, dy=-hy),
        )

    def z_copy(index, part):
        source = [None, 0, 0, 1, 2, 3, 4, 5, 6][index]
        rows = pl.ds(*halves[part])
        step = -1 if index in (1, 3, 5, 7) else 1
        return remote(
            xb.at[2 * source, rows, :], xb.at[2 * min(index, 7), rows, :],
            z_send.at[index, part], z_recv.at[index, part], device(dz=step),
        )

    def z_part(index, n):
        return n if index % 2 else 1 - n

    def c_copy(slot):
        return remote(
            xb.at[2 * slot, body_rows, :], xb.at[2 * slot + 1, body_rows, :], c_send.at[slot], c_recv.at[slot],
            device(dc=1),
        )

    def turn(index):
        rows = pl.ds(index * points, points)
        la[rows, 0:width] = xa[index, 0:width, :].T
        extra = xa[index, aug_at:hi_at, :].astype(f32)
        extra = jnp.concatenate([extra[8:16], extra[0:8], jnp.zeros((112, points), f32)], axis=0)
        la[rows, width:deep] = extra.T.astype(bf16)

    for n in (0, 1):
        for index in (1, 2):
            z_copy(index, z_part(index, n)).start()
        for index in (0, 1, 2):
            a_copy(index, n).start()
    c_copy(0).start()

    turn(own)
    xb[:, rows_sent:deep, :] = jnp.zeros((16, deep - rows_sent, points), bf16)
    acc_a[...] = jnp.zeros_like(acc_a)
    acc_b[...] = jnp.zeros_like(acc_b)
    fetch[2].wait()
    fetch[3].wait()
    rest = res_ref[...]
    empty = jnp.zeros((8, 96), f32)
    old[0] = jnp.concatenate([pack(nt(rest, rest, highest)), empty], axis=1)

    def split(lhs, z_blocks):
        parts = [jnp.dot(lhs, xb[block], preferred_element_type=f32) for block in z_blocks]
        values = jnp.exp(jnp.concatenate(parts, axis=1) * scale)
        high = values.astype(bf16)
        return high, ((values - high.astype(f32)) * low_scale).astype(f8)

    def apply_rows(rows, right, right_low, high, low):
        acc_a[rows, 0:32] += nt(high, right)
        acc_a[rows, 32:64] += nt(low, right_low)

    def directions(z_blocks):
        right = jnp.concatenate([xb[block, hi_at:rows_sent, :] for block in z_blocks], axis=1)
        return right, low_parts(right)

    def both(*z_slots):
        return [block for k in z_slots for block in (2 * k, 2 * k + 1)]

    def tile(first_slots, z_blocks):
        runs = [(first * points, count * points) for first, count in first_slots]
        lhs = [la[pl.ds(*run), :] for run in runs]
        high, low = split(jnp.concatenate(lhs, axis=0) if len(lhs) > 1 else lhs[0], z_blocks)
        right, right_low = directions(z_blocks)
        start = 0
        for run in runs:
            part = slice(start, start + run[1])
            apply_rows(pl.ds(*run), right, right_low, high[part], low[part])
            start += run[1]
        left = [xa[first + n, hi_at:rows_sent, :] for first, count in first_slots for n in range(count)]
        left = jnp.concatenate(left, axis=1) if len(left) > 1 else left[0]
        by_high = jnp.dot(left, high, preferred_element_type=f32)
        by_low = jnp.dot(low_parts(left), low, preferred_element_type=f32)
        for n, block in enumerate(z_blocks):
            lanes = slice(n * points, (n + 1) * points)
            acc_b[block, 0:32, :] += by_high[:, lanes]
            acc_b[block, 32:64, :] += by_low[:, lanes]

    def own_tile(z_blocks):
        rows = pl.ds(own * points, points)
        apply_rows(rows, *directions(z_blocks), *split(la[rows, :], z_blocks))

    low_x, low_y = x < 2, y < 2
    mine = jnp.where(low_x, 0, 1)
    mine_other = jnp.where(low_x == low_y, 0, 1)

    def b_copy(slot):
        return remote(
            part_b.at[slot], sum_b.at[slot], pb_send.at[slot], pb_recv.at[slot],
            device(dz=along_z[slot // 2], dc=slot % 2),
        )

    def hand_b(*which):
        for k in which:
            for slot in (2 * k, 2 * k + 1):
                part_b[slot] = combine(acc_b[slot])
                if slot:
                    b_copy(slot).start()

    def pa_copy(index):
        ox, oy = slots[index][0]
        return remote(
            part_a.at[index], sum_a.at[index], pa_send.at[index], pa_recv.at[index], device(dx=ox, dy=oy)
        )

    def hand_a(*which):
        for index in which:
            part_a[index] = combine(acc_a[pl.ds(index * points, points), :].T)
            if index != own:
                pa_copy(index).start()

    def sum_copies(sent, landed, send, recv):
        plane = sorted(range(1, 16), key=lambda o: -min(o // 4, 4 - o // 4) - min(o % 4, 4 - o % 4))
        column = sorted(range(1, 16), key=lambda o: -min(o // 2, 8 - o // 2))
        targets = [device(dx=o // 4, dy=o % 4) for o in plane]
        targets += [device(dz=o // 2, dc=o % 2) for o in column]
        return [
            remote(sent.at[n // 15], landed.at[n], send.at[n], recv.at[n], to) for n, to in enumerate(targets)
        ]

    def start_stage(copies, stage):
        for copy in copies[15 * stage : 15 * stage + 15]:
            copy.start()

    def finish_stage(copies, sent, landed, stage):
        total = sent[stage]
        for n in range(15 * stage, 15 * stage + 15):
            copies[n].wait_recv()
            total = total + landed[n]
        return total

    old_copies = sum_copies(old, old_in, o_send, o_recv)
    gram_copies = sum_copies(gram, gram_in, g_send, g_recv)
    curv_copies = sum_copies(curv, curv_in, q_send, q_recv)

    def relay(n, z_in, z_out, a_in, a_out):
        for index in z_in:
            z_copy(index, z_part(index, n)).wait_recv()
        for index in z_out:
            z_copy(index, z_part(index, n)).start()
        if n == 1:
            for slot in z_in:
                c_copy(slot).start()
        for index in a_in:
            a_copy(index, n).wait_recv()
            for onward in a_out:
                if parent(onward) == index:
                    a_copy(onward, n).start()

    def siblings(*which):
        for slot in which:
            c_copy(slot).wait_recv()

    def old_first():
        start_stage(old_copies, 0)

    def old_second():
        old[1] = finish_stage(old_copies, old, old_in, 0)
        start_stage(old_copies, 1)

    for n in (0, 1):
        relay(n, (1, 2), (3, 4), (0, 1, 2), (7, 4, 5, 6))
    for index in (0, 1, 2):
        turn(index)
    siblings(0)
    tile([(0, 3)], both(0))
    relay(0, (3, 4), (5, 6), (7, 4, 5, 6), (3, 8))
    siblings(1, 2)
    own_tile(both(0, 1))
    tile([(0, 3)], both(1, 2))
    relay(1, (3, 4), (5, 6), (7, 4, 5, 6), (3, 8))
    for index in (4, 5):
        turn(index)
    tile([(4, 2)], both(0, 1, 2))
    relay(0, (5, 6), (7, 8), (3, 8), ())
    old_first()
    siblings(3, 4)
    tile([(0, 2), (4, 2)], both(3, 4))
    relay(1, (5, 6), (), (3, 8), ())
    turn(3)
    tile([(3, 1)], both(0, 1, 2))
    hand_b(2)
    tile([(2, 2)], both(3, 4))
    hand_b(4)
    for index in (7, 8):
        z_copy(index, z_part(index, 0)).wait_recv()
    c_copy(7).start()
    siblings(5, 6)
    tile([(0, 2), (4, 2)], both(5, 6))
    old_second()
    turn(8)
    tile([(8, 1)], both(1, 3))
    siblings(7)
    tile([(0, 6)], both(7))
    turn(6)
    turn(7)
    hand_a(4, 5, 0, 1)
    tile([(8, 1)], both(5) + [mine, 14 + mine])
    hand_a(8)
    tile([(6, 2)], both(5) + [mine_other, 14 + mine_other])
    hand_b(7, 0)
    tile([(2, 2)], both(5, 6))
    hand_a(3, 2)
    hand_b(5, 6)
    tile([(6, 2)], both(1, 3))
    hand_a(6, 7)
    hand_b(3, 1)
    own_tile(both(2, 3, 4))
    own_tile(both(5, 6, 7))
    hand_a(own)

    ways = [
        xa[index, hi_at:lo_at, :].astype(f32) + xa[index, lo_at:rows_sent, :].astype(f32) for index in others
    ]
    partials = [part_a[index] for index in others]
    held = nt(jnp.concatenate(ways, axis=1), jnp.concatenate(partials, axis=1), highest)
    held = held + 0.5 * nt(way, part_a[own] + ridge_weight * way, highest)
    curv[0] = jnp.concatenate([pack(held + held.T), empty], axis=1)
    start_stage(curv_copies, 0)

    product = part_a[own] + part_b[0] + ridge_weight * way
    for slot in (4, 5, 8, 9, 14, 15, 1, 10, 11, 12, 13):
        b_copy(slot).wait_recv()
        product = product + sum_b[slot]
    for index in (0, 1, 4, 5, 8, 2, 3, 6, 7):
        pa_copy(index).wait_recv()
        product = product + sum_a[index]
    for slot in (2, 3, 6, 7):
        b_copy(slot).wait_recv()
        product = product + sum_b[slot]

    with_rest = nt(product, jnp.concatenate([product, rest], axis=0), highest)
    gram[0] = jnp.concatenate([pack(with_rest[:, 16:32]), pack(with_rest[:, 0:16]), empty[:, 0:64]], axis=1)
    start_stage(gram_copies, 0)
    curv[1] = finish_stage(curv_copies, curv, curv_in, 0)
    start_stage(curv_copies, 1)
    rr = unpack(finish_stage(old_copies, old, old_in, 1), 0)
    rr_inv = inverse(rr)
    for index in others:
        pa_copy(index).wait_send()
        for part in (0, 1):
            a_copy(index, part).wait_send()
    for index in range(1, 9):
        for n in (0, 1) if index < 7 else (0,):
            z_copy(index, z_part(index, n)).wait_send()
    for slot in range(8):
        c_copy(slot).wait_send()
    for slot in range(1, 16):
        b_copy(slot).wait_send()
    for copy in old_copies:
        copy.wait_send()
    gram[1] = finish_stage(gram_copies, gram, gram_in, 0)
    start_stage(gram_copies, 1)

    curvature_inv = inverse(unpack(finish_stage(curv_copies, curv, curv_in, 1), 0))
    alpha_t = nn(rr, curvature_inv)
    turned = nn(jnp.concatenate([curvature_inv, rr_inv], axis=0), way)
    residual_next = rest - nn(alpha_t, product)
    out[16:32] = residual_next
    out[0:16] = sol_ref[...] + nn(alpha_t, way)
    moved = residual_next + way

    for copy in curv_copies + gram_copies[:15]:
        copy.wait_send()
    total = finish_stage(gram_copies, gram, gram_in, 1)
    pr, pp = unpack(total, 0), unpack(total, 32)
    inner = nn(jnp.concatenate([pp, -pr], axis=1), turned)
    out[32:48] = moved + nn(alpha_t, inner) - nn(pr.T, turned[0:16])
    for copy in gram_copies[15:]:
        copy.wait_send()


def shards(embeddings, solution, residual, direction):
    vmem = pl.BlockSpec(memory_space=pltpu.VMEM)
    dma = pltpu.SemaphoreType.DMA
    stacked = pl.pallas_call(
        kernel,
        out_shape=jax.ShapeDtypeStruct((3 * rubrics, points), f32),
        in_specs=[pl.BlockSpec(memory_space=pl.ANY)] * 4,
        out_specs=vmem,
        scratch_shapes=[
            pltpu.VMEM((width, points), bf16),
            pltpu.VMEM((rubrics, points), f32),
            pltpu.VMEM((rubrics, points), f32),
            pltpu.VMEM((rubrics, points), f32),
            pltpu.VMEM((16, deep, points), bf16),
            pltpu.VMEM((10, rows_sent, points), bf16),
            pltpu.VMEM((10 * points, deep), bf16),
            pltpu.VMEM((10 * points, 64), f32),
            pltpu.VMEM((16, 64, points), f32),
            pltpu.VMEM((10, rubrics, points), f32),
            pltpu.VMEM((16, rubrics, points), f32),
            pltpu.VMEM((10, rubrics, points), f32),
            pltpu.VMEM((16, rubrics, points), f32),
            pltpu.VMEM((2, 8, 128), f32),
            pltpu.VMEM((30, 8, 128), f32),
            pltpu.VMEM((2, 8, 128), f32),
            pltpu.VMEM((30, 8, 128), f32),
            pltpu.VMEM((2, 8, 128), f32),
            pltpu.VMEM((30, 8, 128), f32),
            dma((4,)), dma((10, 2)), dma((10, 2)), dma((9, 2)), dma((9, 2)), dma((8,)), dma((8,)),
            dma((10,)), dma((10,)), dma((16,)), dma((16,)), dma((30,)), dma((30,)), dma((30,)), dma((30,)),
            dma((30,)), dma((30,)),
        ],
        compiler_params=pltpu.CompilerParams(
            collective_id=0, has_side_effects=True, vmem_limit_bytes=56 * 2**20
        ),
        cost_estimate=pl.CostEstimate(
            flops=20_000_000_000, bytes_accessed=1_000_000, transcendentals=9_000_000
        ),
        name="iteration",
    )(embeddings, solution, residual, direction)
    return stacked[0:16], stacked[16:32], stacked[32:48]


def solution(mesh):
    spec = P(None, ("row", "col"))
    return jax.shard_map(
        shards, mesh=mesh, in_specs=(spec,) * 4, out_specs=(spec,) * 3, check_vma=False
    )
```
